128 devices in a mesh: tm: 8 (over z, y_lo), rowblk: 4 (over y_hi, core), colblk: 4 (over x).
Axes of the slice: x: 4, y: 4 (y_hi: 2, y_lo: 2; y = y_hi * 2 + y_lo), z: 4, core: 2. Of those that a mesh axis runs over, the one named last changes fastest.
Arguments:
- signal: bfloat16 [6144, 16384], P('tm', ('rowblk', 'colblk')), may hold values from -180 to 180
- tile_owner: int32 [128], replicated, may hold values from 0 to 15, as said below
Outputs:
- covariance: float32 [16, 16, 8, 128, 512], P(('rowblk', 'colblk'), 'tm')
The draws below stay inside these ranges and needn't reach their ends.
Inputs may be any that keep to these rules, and one draw needn't show every extreme that they name: `tile_owner`: each channel block's tiles go to distinct owners (at most one tile of a block to one owner); every owner has between 4 and 16 first tiles, and some owner exactly 16.
All inputs are finite; a program needn't handle non-finite values.
Results may differ from the reference program's by a relative error of at most 0.015.
Values may be sent and summed in bfloat16 or wider, within the bound.
A program may use at most 128 MiB of HBM per device.

```python
import jax
import jax.numpy as jnp
import numpy as np
from jax import lax

TILE = 128
CH = 16384
SEG = 768
LAGS = 8
APER = 3
OCAP = 16
OWNERS = 16
NT = 128
TIME = 6144
N_TM = 8


load_pattern = (16, 16, 12, 12, 8, 8, 8, 8, 6, 6, 6, 6, 4, 4, 4, 4)


def draw_signal(key, part):
    key = jax.random.fold_in(key, 11)
    key_noise, key_scale = jax.random.split(key, 2)
    scales = jnp.exp(jax.random.uniform(key_scale, (1, CH), jnp.float32) * jnp.log(10.0))
    ramp = jnp.arange(TIME, dtype=jnp.float32)[:, None] / max(TIME - 1, 1)
    noise = jnp.clip(jax.random.normal(key_noise, (TIME, CH), jnp.float32), -6.0, 6.0)
    envelope = 1.0 + 2.0 * ramp
    values = noise * scales * envelope
    return values.astype(jnp.bfloat16)


def draw_tile_owner(key, part):
    key = jax.random.fold_in(key, 5)
    key_owner, key_place = jax.random.split(key)
    groups = jnp.array(np.repeat(np.arange(16), load_pattern), jnp.int32)
    owner_order = jax.random.permutation(key_owner, 16).astype(jnp.int32)
    token_owner = owner_order[groups]

    def shuffle(subkey):
        return jax.random.permutation(subkey, 8).astype(jnp.int32)
    positions = jax.vmap(shuffle)(jax.random.split(key_place, 16))
    token_index = jnp.arange(NT, dtype=jnp.int32)
    source = token_index % 16
    slot_index = token_index // 16
    tile_index = source * 8 + positions[source, slot_index]
    return jnp.zeros((NT,), jnp.int32).at[tile_index].set(token_owner)


def setup_inputs(seed: int = 0) -> dict:
    key_list = jax.random.split(jax.random.key(seed), 3)
    signal = draw_signal(jax.random.fold_in(key_list[2], 71), 0)
    tile_owner = draw_tile_owner(jax.random.fold_in(key_list[2], 71), 0)
    return dict(signal=signal, tile_owner=tile_owner)


def reference(signal, tile_owner):
    values = signal.astype(jnp.float32)
    power_sum = lax.optimization_barrier(jnp.sum(values * values, axis=0))
    normed = (values * lax.rsqrt(power_sum / TIME + 1e-06)).astype(jnp.bfloat16)
    padded = jnp.pad(normed, ((0, LAGS - 1), (0, APER * TILE)))
    win_width = (APER + 1) * TILE

    def one_tile(tile_pos):
        column = (tile_pos * TILE).astype(jnp.int32)
        first_tile = lax.dynamic_slice(padded, (jnp.int32(0), column), (TIME, TILE))
        first_tile = first_tile.astype(jnp.float32).reshape(N_TM, SEG, TILE)
        lag_terms = []
        for lag_step in range(LAGS):
            second = lax.dynamic_slice(padded, (jnp.int32(lag_step), column), (TIME, win_width))
            second = second.astype(jnp.float32).reshape(N_TM, SEG, win_width)
            seg_term = jnp.einsum('nsi,nsc->nic', first_tile, second).astype(jnp.bfloat16)
            seg_term = lax.optimization_barrier(seg_term).astype(jnp.float32)
            lag_terms.append(lax.optimization_barrier(jnp.sum(seg_term, axis=0)))
        return jnp.stack(lag_terms, axis=0) * lax.rsqrt(jnp.float32(TIME))
    results = lax.map(one_tile, jnp.arange(NT, dtype=jnp.int32))
    owner_hot = (tile_owner[:, None] == jnp.arange(OWNERS, dtype=jnp.int32)[None, :]).astype(jnp.int32)
    earlier = jnp.cumsum(owner_hot, axis=0) - owner_hot
    slot_index = lax.optimization_barrier(jnp.sum(earlier * owner_hot, axis=1)).astype(jnp.int32)
    covariance = jnp.zeros((OWNERS, OCAP, LAGS, TILE, win_width), jnp.float32)
    return covariance.at[tile_owner, slot_index].set(results)
```

```python
import jax
import jax.numpy as jnp
from jax import lax
from jax.sharding import PartitionSpec as P

TILE = 128
LAGS = 8
APER = 3
OCAP = 16


def passed_along(block, axis, distance):
    devices = range(lax.axis_size(axis))
    route = [(i - distance, i) for i in devices if i - distance in devices]
    return lax.ppermute(block, axis, route)


def shards(signal, tile_owner):
    seg_rows, local_width = signal.shape
    tiles_here = local_width // TILE
    owners = lax.axis_size(("rowblk", "colblk"))
    segments = lax.axis_size("tm")
    total_time = seg_rows * segments
    win_width = (APER + 1) * TILE
    values = signal.astype(jnp.float32)
    power_sum = lax.psum(jnp.sum(values * values, axis=0), "tm")
    normed = (values * lax.rsqrt(power_sum / total_time + 1e-06)).astype(jnp.bfloat16)
    following = passed_along(normed[:, : APER * TILE], ("rowblk", "colblk"), -1)
    extended = jnp.concatenate([normed, following], axis=1)
    my_index = lax.axis_index(("rowblk", "colblk"))
    owner_table = tile_owner.reshape(owners, tiles_here)
    my_owners = lax.dynamic_index_in_dim(owner_table, my_index, 0, keepdims=False)
    targets = jnp.arange(owners, dtype=jnp.int32)
    matches = my_owners[None, :] == targets[:, None]
    local_pos = jnp.sum(
        jnp.where(matches, jnp.arange(tiles_here, dtype=jnp.int32)[None, :], 0), axis=1
    )
    arrived = jnp.any(owner_table == my_index, axis=1)
    slot_rank = jnp.cumsum(arrived.astype(jnp.int32)) - 1
    picker = (slot_rank[None, :] == jnp.arange(OCAP, dtype=jnp.int32)[:, None]) & arrived[None, :]
    source_of = jnp.sum(jnp.where(picker, targets[None, :], 0), axis=1)
    filled = jnp.any(picker, axis=1)

    windows = jnp.stack(
        [extended[:, a * TILE : a * TILE + win_width] for a in range(tiles_here)], axis=0
    )
    window = lax.all_to_all(windows, "tm", split_axis=0, concat_axis=0, tiled=True)
    window = window.reshape(total_time, win_width)
    later = jnp.pad(window, ((0, LAGS - 1), (0, 0)))
    first = window[:, :TILE]
    result = jnp.stack(
        [
            jnp.einsum(
                "ti,tc->ic", first, later[l : l + total_time], preferred_element_type=jnp.float32
            )
            for l in range(LAGS)
        ],
        axis=0,
    )
    result = (result * lax.rsqrt(jnp.float32(total_time))).astype(jnp.bfloat16)
    by_lag = lax.all_to_all(result, "tm", split_axis=0, concat_axis=0, tiled=True)
    outgoing = jnp.take(by_lag, local_pos, axis=0)
    incoming = lax.all_to_all(
        outgoing, ("rowblk", "colblk"), split_axis=0, concat_axis=0, tiled=True
    )
    slots = jnp.where(
        filled[:, None, None], jnp.take(incoming, source_of, axis=0), jnp.zeros((), jnp.bfloat16)
    )
    mine = lax.all_to_all(slots, "tm", split_axis=0, concat_axis=0, tiled=True)
    mine = mine.reshape(LAGS, OCAP // segments, TILE, win_width).transpose(1, 0, 2, 3)
    return mine.astype(jnp.float32)[None]


def solution(mesh):
    return jax.shard_map(
        shards,
        mesh=mesh,
        in_specs=(P("tm", ("rowblk", "colblk")), P()),
        out_specs=P(("rowblk", "colblk"), "tm", None, None, None),
        check_vma=False,
    )
```

```python
import functools

import jax
import jax.numpy as jnp
from jax import lax
from jax.experimental import pallas as pl
from jax.experimental.pallas import tpu as pltpu
from jax.sharding import PartitionSpec as P

MESH = pl.DeviceIdType.MESH
TILE = 128
LAGS = 8
APER = 3
OCAP = 16
BLOCKS = 16
SEGS = 8
ROWS = 768
WIN = 512
HALF = 256
HALO = 16
PRESCALE = 2.0**40


def kernel(
    pos_ref, src_ref, fill_ref, sig_ref, out_ref,
    ybuf, halo, amat, acc, pow_mine, pow_other, send_y, recv_y, send_z,
    piece_a, piece_b, send_o, recv_o_a, recv_o_b, send_t,
    g_send, g_recv, h_send, h_recv, p_send, p_recv, y_send, y_recv,
    z_send, z_recv, o_send, o_recv, t_send, t_recv,
):
    t = lax.axis_index("tm")
    row = lax.axis_index("rowblk")
    col = lax.axis_index("colblk")
    b = row * 4 + col
    z = t // 2
    yl = t % 2

    piece = (piece_a, piece_b)
    recv_o = (recv_o_a, recv_o_b)

    def dev(block, tm):
        return (tm, block // 4, block % 4)

    barrier = pltpu.get_barrier_semaphore()
    for d in range(1, SEGS):
        pl.semaphore_signal(barrier, inc=1, device_id=dev(b, (t + d) % SEGS), device_id_type=MESH)
    for d in range(1, BLOCKS):
        pl.semaphore_signal(barrier, inc=1, device_id=dev((b + d) % BLOCKS, t), device_id_type=MESH)
    for d in (1, BLOCKS - 1):
        for k in range(1, 4):
            pl.semaphore_signal(
                barrier, inc=1, device_id=dev((b + d) % BLOCKS, (t + 2 * k) % SEGS), device_id_type=MESH
            )
    pl.semaphore_wait(barrier, SEGS - 1 + BLOCKS - 1 + 6)

    def window_copy(k, c):
        zd = (z + k) % 4
        tile = 2 * zd + c
        block = (b + BLOCKS - tile // 8) % BLOCKS
        src = sig_ref.at[:, pl.ds(pl.multiple_of((tile % 8) * TILE, TILE), TILE)]
        dst = ybuf.at[z, :, pl.ds(c * TILE, TILE)]
        return src, dst, block, zd

    def start_window(k, c):
        src, dst, block, zd = window_copy(k, c)
        pltpu.make_async_remote_copy(
            src_ref=src, dst_ref=dst, send_sem=g_send.at[k, c], recv_sem=g_recv.at[z, c],
            device_id=dev(block, 2 * zd + yl), device_id_type=MESH,
        ).start()

    def local_window(c):
        src, dst, _, _ = window_copy(0, c)
        return pltpu.make_async_copy(src, dst, g_recv.at[z, c])

    def wait_window_recv(s, c):
        dst = ybuf.at[s, :, pl.ds(c * TILE, TILE)]
        pltpu.make_async_remote_copy(
            src_ref=dst, dst_ref=dst, send_sem=g_send.at[0, c], recv_sem=g_recv.at[s, c],
            device_id=dev(b, (t + 1) % SEGS), device_id_type=MESH,
        ).wait_recv()

    def wait_window_send(k, c):
        src, dst, block, zd = window_copy(k, c)
        pltpu.make_async_remote_copy(
            src_ref=src, dst_ref=dst, send_sem=g_send.at[k, c], recv_sem=g_recv.at[z, c],
            device_id=dev((b + 1) % BLOCKS, 2 * zd + yl), device_id_type=MESH,
        ).wait_send()

    def own(c):
        return 2 * z + c < 8

    def start_windows(tiles):
        for c in tiles:
            for k in (2, 1, 3):
                start_window(k, c)
            if c < 2:
                local_window(c).start()
            else:
                pl.when(own(c))(lambda c=c: local_window(c).start())
                pl.when(jnp.logical_not(own(c)))(lambda c=c: start_window(0, c))

    def wait_windows(k, tiles):
        s = (z + k) % 4
        for c in tiles:
            if k == 0:
                if c < 2:
                    local_window(c).wait()
                else:
                    pl.when(own(c))(lambda c=c: local_window(c).wait())
                    pl.when(jnp.logical_not(own(c)))(lambda c=c: wait_window_recv(s, c))
            else:
                wait_window_recv(s, c)

    def halo_copy(k):
        zd = (z + k) % 4
        slot = (z + yl) % 4
        return pltpu.make_async_remote_copy(
            src_ref=sig_ref.at[pl.ds(ROWS - HALO, HALO), pl.ds(pl.multiple_of(zd * HALF, HALF), HALF)],
            dst_ref=halo.at[slot], send_sem=h_send.at[k], recv_sem=h_recv.at[slot],
            device_id=dev(b, 2 * zd + 1 - yl), device_id_type=MESH,
        )

    def wait_halo(s):
        pltpu.make_async_remote_copy(
            src_ref=halo.at[s], dst_ref=halo.at[s], send_sem=h_send.at[0], recv_sem=h_recv.at[s],
            device_id=dev(b, (t + 1) % SEGS), device_id_type=MESH,
        ).wait_recv()

    for k in range(4):
        halo_copy(k).start()
    start_windows((0, 1, 2))
    start_windows((3, 4))

    def square_sums(s, part):
        first, width = (0, 3 * TILE) if part == 0 else (3 * TILE, 2 * TILE)
        v = ybuf[s, :, first : first + width].astype(jnp.float32)
        total = jnp.sum((v * v).reshape(ROWS // 8, 8, width), axis=0)
        pow_mine[part, :, 0:width] = pow_mine[part, :, 0:width] + total

    def build_lags(s):
        keep = jnp.where(jnp.logical_and(s == 0, yl == 0), 0.0, PRESCALE)
        for a in range(2):
            x = ybuf[s, :, a * TILE : (a + 1) * TILE].astype(jnp.float32) * PRESCALE
            h = halo[s, :, a * TILE : (a + 1) * TILE].astype(jnp.float32) * keep
            rows = jnp.concatenate([jnp.zeros((TILE - HALO, TILE), jnp.float32), h, x], axis=0)
            cols = jnp.transpose(rows)
            for j in range(LAGS):
                shifted = cols if j == 0 else pltpu.roll(cols, j, 1)
                amat[s, a, j * TILE : (j + 1) * TILE, :] = shifted[:, TILE:].astype(jnp.bfloat16)

    def products(s, part, first):
        for a in range(2):
            y = ybuf[s, :, (a + 2 * part) * TILE : (a + 2 * part + 2) * TILE]
            for j in range(0, LAGS, 2):
                p = jnp.dot(
                    amat[s, a, j * TILE : (j + 2) * TILE, :], y, preferred_element_type=jnp.float32
                ).reshape(2, TILE, HALF)
                if first:
                    acc[part, a, j : j + 2] = p
                else:
                    acc[part, a, j : j + 2] = acc[part, a, j : j + 2] + p

    pow_mine[...] = jnp.zeros_like(pow_mine)

    def partner_power(part):
        return pltpu.make_async_remote_copy(
            src_ref=pow_mine.at[part], dst_ref=pow_other.at[part], send_sem=p_send.at[part],
            recv_sem=p_recv.at[part], device_id=dev(b, 2 * z + 1 - yl), device_id_type=MESH,
        )

    def partner_terms(part):
        return pltpu.make_async_remote_copy(
            src_ref=send_y.at[part], dst_ref=recv_y.at[part], send_sem=y_send.at[part],
            recv_sem=y_recv.at[part], device_id=dev(b, 2 * z + 1 - yl), device_id_type=MESH,
        )

    def start_partner(part):
        partner_power(part).start()
        for a in range(2):
            for q in range(4):
                send_y[part, a, q] = acc[part, a, 2 * q + 1 - yl].astype(jnp.bfloat16)
        partner_terms(part).start()

    def channel_scale(part):
        total = jnp.sum(pow_mine[part] + pow_other[part], axis=0, keepdims=True)
        return lax.rsqrt(total * (1.0 / (SEGS * ROWS)) + 1e-06)

    def piece_copy(part, k):
        zd = (z + k) % 4
        return pltpu.make_async_remote_copy(
            src_ref=send_z.at[part, zd], dst_ref=piece[part].at[pl.ds(2 * z, 2)],
            send_sem=z_send.at[part, k], recv_sem=z_recv.at[part, z],
            device_id=dev(b, 2 * zd + yl), device_id_type=MESH,
        )

    def wait_piece(part, k):
        s = (z + k) % 4
        pltpu.make_async_remote_copy(
            src_ref=send_z.at[part, s], dst_ref=piece[part].at[pl.ds(2 * s, 2)],
            send_sem=z_send.at[part, k], recv_sem=z_recv.at[part, s],
            device_id=dev(b, 2 * s + yl), device_id_type=MESH,
        ).wait_recv()

    def start_pieces(part):
        partner_power(part).wait_recv()
        scales = channel_scale(part)
        if part == 0:
            low = scales
            wide = scales
        else:
            low = channel_scale(0)
            wide = jnp.concatenate([low[:, 2 * TILE :], scales[:, : 2 * TILE]], axis=1)
        first = 2 * z + 2 * part
        lane_tile = lax.broadcasted_iota(jnp.int32, (1, 3 * TILE), 1) // TILE + first
        last_block = jnp.broadcast_to(b, (1, 3 * TILE)) == BLOCKS - 1
        wide = jnp.where(jnp.logical_and(lane_tile >= 8, last_block), 0.0, wide)
        norm = (1.0 / PRESCALE) * float(SEGS * ROWS) ** -0.5
        partner_terms(part).wait_recv()
        for a in range(2):
            rows_scale = jnp.transpose(
                jnp.broadcast_to(low[:, a * TILE : (a + 1) * TILE] * norm, (TILE, TILE))
            )
            rows_scale = jnp.concatenate([rows_scale, rows_scale], axis=1)
            both = rows_scale * wide[:, a * TILE : (a + 2) * TILE]
            for q in range(4):
                total = acc[part, a, 2 * q + yl] + recv_y[part, a, q].astype(jnp.float32)
                send_z[part, q, a] = (total * both).astype(jnp.bfloat16)
        for k in (2, 1, 3):
            piece_copy(part, k).start()
        piece[part][pl.ds(2 * z, 2)] = send_z[part, z]

    def owner_copy(part, d):
        o = (b + d) % BLOCKS
        return pltpu.make_async_remote_copy(
            src_ref=send_o.at[part, d], dst_ref=recv_o[part].at[b], send_sem=o_send.at[part, d],
            recv_sem=o_recv.at[part, b], device_id=dev(o, t), device_id_type=MESH,
        )

    def wait_owner(part, d):
        s = (b + d) % BLOCKS
        pltpu.make_async_remote_copy(
            src_ref=send_o.at[part, d], dst_ref=recv_o[part].at[s], send_sem=o_send.at[part, d],
            recv_sem=o_recv.at[part, s], device_id=dev(s, t), device_id_type=MESH,
        ).wait_recv()

    def start_owners(part):
        for k in (1, 3, 2):
            wait_piece(part, k)

        def send(d, _):
            o = (b + d) % BLOCKS
            send_o[part, d] = piece[part][pos_ref[o]]
            owner_copy(part, d).start()
            return 0

        lax.fori_loop(1, BLOCKS, send, 0)
        recv_o[part][b] = piece[part][pos_ref[b]]

    def slot_dst(part, lag):
        return out_ref.at[:, lag, :, pl.ds(part * HALF, HALF)]

    def slot_copy(part, d):
        return pltpu.make_async_remote_copy(
            src_ref=send_t.at[part, d], dst_ref=slot_dst(part, t), send_sem=t_send.at[part, d],
            recv_sem=t_recv.at[part, t], device_id=dev(b, (t + d) % SEGS), device_id_type=MESH,
        )

    def own_slots(part):
        return pltpu.make_async_copy(send_t.at[part, 0], slot_dst(part, t), t_recv.at[part, t])

    def wait_slots(part, d):
        s = (t + d) % SEGS
        pltpu.make_async_remote_copy(
            src_ref=send_t.at[part, d], dst_ref=slot_dst(part, s), send_sem=t_send.at[part, d],
            recv_sem=t_recv.at[part, s], device_id=dev(b, s), device_id_type=MESH,
        ).wait_recv()

    def start_slots(part):
        def arrive(d, _):
            wait_owner(part, d)
            return 0

        lax.fori_loop(1, BLOCKS, arrive, 0)

        def fill(d):
            base = 2 * ((t + d) % SEGS)
            for e in range(2):
                taken = recv_o[part][src_ref[base + e]]
                keep = jnp.broadcast_to(fill_ref[base + e], (TILE, HALF)) > 0
                send_t[part, d, e] = jnp.where(keep, taken.astype(jnp.float32), 0.0).astype(jnp.bfloat16)

        def send(d, _):
            fill(d)
            slot_copy(part, d).start()
            return 0

        lax.fori_loop(1, SEGS, send, 0)
        fill(0)
        own_slots(part).start()

    for k in (0, 1, 3, 2):
        s = (z + k) % 4
        wait_halo(s)
        wait_windows(k, (0, 1, 2))
        build_lags(s)
        products(s, 0, k == 0)
        square_sums(s, 0)
    start_partner(0)
    for k in (0, 1, 3, 2):
        s = (z + k) % 4
        wait_windows(k, (3, 4))
        products(s, 1, k == 0)
        square_sums(s, 1)
    start_partner(1)
    start_pieces(0)
    start_owners(0)
    start_pieces(1)
    start_slots(0)
    start_owners(1)
    start_slots(1)

    for k in range(4):
        halo_copy(k).wait_send()
    for c in range(5):
        for k in (1, 2, 3):
            wait_window_send(k, c)
        if c >= 2:
            pl.when(jnp.logical_not(own(c)))(lambda c=c: wait_window_send(0, c))
    for part in range(2):
        partner_power(part).wait_send()
        partner_terms(part).wait_send()
        for k in (1, 2, 3):
            piece_copy(part, k).wait_send()

        def owner_done(d, _, part=part):
            owner_copy(part, d).wait_send()
            return 0

        lax.fori_loop(1, BLOCKS, owner_done, 0)

        def slot_done(d, _, part=part):
            slot_copy(part, d).wait_send()
            wait_slots(part, d)
            return 0

        lax.fori_loop(1, SEGS, slot_done, 0)
        own_slots(part).wait()


def route(tile_owner):
    owner_table = tile_owner.reshape(BLOCKS, NT_HERE)
    my_index = lax.axis_index(("rowblk", "colblk"))
    my_owners = lax.dynamic_index_in_dim(owner_table, my_index, 0, keepdims=False)
    targets = jnp.arange(BLOCKS, dtype=jnp.int32)
    matches = my_owners[None, :] == targets[:, None]
    local_pos = jnp.sum(
        jnp.where(matches, jnp.arange(NT_HERE, dtype=jnp.int32)[None, :], 0), axis=1
    )
    arrived = jnp.any(owner_table == my_index, axis=1)
    slot_rank = jnp.cumsum(arrived.astype(jnp.int32)) - 1
    picker = (slot_rank[None, :] == jnp.arange(OCAP, dtype=jnp.int32)[:, None]) & arrived[None, :]
    source_of = jnp.sum(jnp.where(picker, targets[None, :], 0), axis=1)
    filled = jnp.any(picker, axis=1).astype(jnp.int32)
    return local_pos, source_of, filled


NT_HERE = 8


def shards(signal, tile_owner):
    local_pos, source_of, filled = route(tile_owner)
    bf16, f32, vmem, dma = jnp.bfloat16, jnp.float32, pltpu.VMEM, pltpu.SemaphoreType.DMA
    out = pl.pallas_call(
        kernel,
        out_shape=jax.ShapeDtypeStruct((2, LAGS, TILE, WIN), bf16),
        in_specs=[pl.BlockSpec(memory_space=pltpu.SMEM)] * 3 + [pl.BlockSpec(memory_space=pl.ANY)],
        out_specs=pl.BlockSpec(memory_space=pl.ANY),
        scratch_shapes=[
            vmem((4, ROWS, 5 * TILE), bf16),
            vmem((4, HALO, HALF), bf16),
            vmem((4, 2, LAGS * TILE, ROWS), bf16),
            vmem((2, 2, LAGS, TILE, HALF), f32),
            vmem((2, 8, 3 * TILE), f32),
            vmem((2, 8, 3 * TILE), f32),
            vmem((2, 2, 4, TILE, HALF), bf16),
            vmem((2, 2, 4, TILE, HALF), bf16),
            vmem((2, 4, 2, TILE, HALF), bf16),
            vmem((8, TILE, HALF), bf16),
            vmem((8, TILE, HALF), bf16),
            vmem((2, BLOCKS, TILE, HALF), bf16),
            vmem((BLOCKS, TILE, HALF), bf16),
            vmem((BLOCKS, TILE, HALF), bf16),
            vmem((2, SEGS, 2, TILE, HALF), bf16),
            dma((4, 5)), dma((4, 5)), dma((4,)), dma((4,)), dma((2,)), dma((2,)), dma((2,)), dma((2,)),
            dma((2, 4)), dma((2, 4)), dma((2, BLOCKS)), dma((2, BLOCKS)), dma((2, SEGS)), dma((2, SEGS)),
        ],
        compiler_params=pltpu.CompilerParams(
            collective_id=0, has_side_effects=True, vmem_limit_bytes=48 * 1024 * 1024
        ),
    )(local_pos, source_of, filled, signal)
    return out.astype(f32)[None]


def solution(mesh):
    return jax.shard_map(
        shards,
        mesh=mesh,
        in_specs=(P("tm", ("rowblk", "colblk")), P()),
        out_specs=P(("rowblk", "colblk"), "tm", None, None, None),
        check_vma=False,
    )
```

```python
import functools

import jax
import jax.numpy as jnp
from jax import lax
from jax.experimental import pallas as pl
from jax.experimental.pallas import tpu as pltpu
from jax.sharding import PartitionSpec as P

MESH = pl.DeviceIdType.MESH
TILE = 128
LAGS = 8
APER = 3
OCAP = 16
BLOCKS = 16
SEGS = 8
ROWS = 768
WIN = 512
HALF = 256
HALO = 16
PRESCALE = 2.0**40
FORWARDS = ()
FIRST_SENDS = ((2, 0), (1, 0), (3, 0), (2, 1), (1, 1), (3, 1))
LATER_SENDS = (
    ((2, 2), (1, 2), (3, 2), (0, 2), (2, 3), (1, 3), (3, 3), (0, 3), (2, 4), (1, 4), (3, 4), (0, 4)), (), (), (), (),
)


def kernel(
    pos_ref, src_ref, fill_ref, sig_ref, out_ref,
    ybuf, halo, following, amat, acc, pow_mine, pow_other, row_scale, send_y, recv_y, send_z,
    piece_0, piece_1, piece_2, piece_3, recv_o_0, recv_o_1, recv_o_2, recv_o_3, send_o, send_t,
    g_send, g_recv, f_send, n_send, n_recv, h_send, h_recv, p_send, p_recv, y_send, y_recv,
    z_send, z_recv, o_send, o_recv, t_send, t_recv,
):
    t = lax.axis_index("tm")
    row = lax.axis_index("rowblk")
    col = lax.axis_index("colblk")
    b = row * 4 + col
    z = t // 2
    yl = t % 2
    piece = (piece_0, piece_1, piece_2, piece_3)
    recv_o = (recv_o_0, recv_o_1, recv_o_2, recv_o_3)

    def dev(block, tm):
        return (tm, block // 4, block % 4)

    def remote(src, dst, send_sem, recv_sem, device):
        return pltpu.make_async_remote_copy(
            src_ref=src, dst_ref=dst, send_sem=send_sem, recv_sem=recv_sem,
            device_id=device, device_id_type=MESH,
        )

    partner = dev(b, 2 * z + 1 - yl)

    barrier = pltpu.get_barrier_semaphore()
    for d in range(1, SEGS):
        pl.semaphore_signal(barrier, inc=1, device_id=dev(b, (t + d) % SEGS), device_id_type=MESH)
    for d, k in ((1, 2), (BLOCKS - 1, SEGS - 2)):
        pl.semaphore_signal(
            barrier, inc=1, device_id=dev((b + d) % BLOCKS, (t + k) % SEGS), device_id_type=MESH
        )
    for d in range(1, BLOCKS):
        pl.semaphore_signal(barrier, inc=1, device_id=dev((b + d) % BLOCKS, t), device_id_type=MESH)

    def window_dst(c):
        return ybuf.at[z, :, pl.ds(c * TILE, TILE)]

    def own_tile(g):
        return sig_ref.at[:, pl.ds(pl.multiple_of(g * TILE, TILE), TILE)]

    def window_copy(k, c, src):
        zd = (z + k) % 4
        return remote(src, window_dst(c), g_send.at[k, c], g_recv.at[z, c], dev(b, 2 * zd + yl))

    def start_window(k, c):
        g = 2 * ((z + k) % 4) + c

        def start(src):
            if k == 0:
                pltpu.make_async_copy(src, window_dst(c), g_recv.at[z, c]).start()
            else:
                window_copy(k, c, src).start()

        if c < 2:
            start(own_tile(g))
        else:
            pl.when(g < 8)(lambda: start(own_tile(g)))
            pl.when(g >= 8)(lambda: start(following.at[g - 8]))

    def wait_window(k, c):
        s = (z + k) % 4
        dst = ybuf.at[s, :, pl.ds(c * TILE, TILE)]
        if k == 0:
            pltpu.make_async_copy(dst, dst, g_recv.at[s, c]).wait()
        else:
            remote(dst, dst, g_send.at[k, c], g_recv.at[s, c], partner).wait_recv()

    def following_copy(i):
        return remote(
            own_tile(i), following.at[i], n_send.at[i], n_recv.at[i], dev((b + BLOCKS - 1) % BLOCKS, t)
        )

    def forward(c):
        step, held = (1, 3) if c == 1 else (3, c - 2)
        s = (z + 3) % 4 if c == 1 else (z + 1) % 4
        zd = (z + step) % 4
        block = (b + (z + step) // 4 + (BLOCKS if c == 1 else BLOCKS - 1)) % BLOCKS
        return remote(
            ybuf.at[s, :, pl.ds(held * TILE, TILE)], ybuf.at[s, :, pl.ds(c * TILE, TILE)],
            f_send.at[c - 1], g_recv.at[s, c], dev(block, 2 * zd + yl),
        )

    def halo_copy(k):
        zd = (z + k) % 4
        slot = (z + yl) % 4
        src = sig_ref.at[pl.ds(ROWS - HALO, HALO), pl.ds(pl.multiple_of(zd * HALF, HALF), HALF)]
        return remote(src, halo.at[slot], h_send.at[k], h_recv.at[slot], dev(b, 2 * zd + 1 - yl))

    def wait_halo(s):
        remote(halo.at[s], halo.at[s], h_send.at[0], h_recv.at[s], partner).wait_recv()

    for c in range(2):
        start_window(0, c)

    pl.semaphore_wait(barrier, SEGS - 1 + BLOCKS - 1 + 2)

    for k in range(4):
        halo_copy(k).start()
    for i in range(APER):
        following_copy(i).start()
    for k, c in FIRST_SENDS:
        start_window(k, c)

    def square_sums(s, c, first):
        v = ybuf[s, :, c * TILE : (c + 1) * TILE].astype(jnp.float32)
        total = jnp.sum((v * v).reshape(ROWS // 8, 8, TILE), axis=0)
        pow_mine[c] = total if first else pow_mine[c] + total

    def build_lags(s, a):
        keep = jnp.where(jnp.logical_and(s == 0, yl == 0), 0.0, PRESCALE)
        x = ybuf[s, :, a * TILE : (a + 1) * TILE].astype(jnp.float32) * PRESCALE
        h = halo[s, :, a * TILE : (a + 1) * TILE].astype(jnp.float32) * keep
        rows = jnp.concatenate([jnp.zeros((TILE - HALO, TILE), jnp.float32), h, x], axis=0)
        cols = jnp.transpose(rows)
        for j in range(LAGS):
            shifted = cols if j == 0 else pltpu.roll(cols, j, 1)
            amat[s, a, j * TILE : (j + 1) * TILE, :] = shifted[:, TILE:].astype(jnp.bfloat16)

    def products(s, c, first):
        y = ybuf[s, :, c * TILE : (c + 1) * TILE]
        for a in range(2):
            d = c - a
            if 0 <= d < 4:
                p = jnp.dot(amat[s, a], y, preferred_element_type=jnp.float32)
                p = p.reshape(LAGS, TILE, TILE)
                acc[d, a] = p if first else acc[d, a] + p

    def partner_power(c):
        return remote(pow_mine.at[c], pow_other.at[c], p_send.at[c], p_recv.at[c], partner)

    def partner_terms(d, a):
        return remote(send_y.at[d, a], recv_y.at[d, a], y_send.at[d, a], y_recv.at[d, a], partner)

    def compute(c):
        for k in (0, 1, 3, 2):
            s = (z + k) % 4
            if c == 0:
                wait_halo(s)
            if c == 1 and k == 2 and 1 in FORWARDS:
                wait_window(3, 3)
                forward(1).start()
            if not (k == 3 and c == 3 and 1 in FORWARDS):
                wait_window(k, c)
            if k == 1 and c + 2 in FORWARDS:
                forward(c + 2).start()
            if c < 2:
                build_lags(s, c)
            products(s, c, k == 0)
            square_sums(s, c, k == 0)
        if c == 0:
            for i in range(APER):
                following_copy(i).wait_recv()
        for k, e in LATER_SENDS[c]:
            start_window(k, e)
        partner_power(c).start()
        for a in range(2):
            d = c - a
            if 0 <= d < 4:
                for q in range(4):
                    send_y[d, a, q] = acc[d, a, 2 * q + 1 - yl].astype(jnp.bfloat16)
                partner_terms(d, a).start()

    def channel_scale(c):
        total = jnp.sum(pow_mine[c] + pow_other[c], axis=0, keepdims=True)
        return lax.rsqrt(total * (1.0 / (SEGS * ROWS)) + 1e-06)

    def piece_copy(d, k):
        zd = (z + k) % 4
        return remote(
            send_z.at[d, zd], piece[d].at[pl.ds(2 * z, 2)], z_send.at[d, k], z_recv.at[d, z],
            dev(b, 2 * zd + yl),
        )

    def wait_piece(d, k):
        s = (z + k) % 4
        remote(
            send_z.at[d, s], piece[d].at[pl.ds(2 * s, 2)], z_send.at[d, k], z_recv.at[d, s], partner
        ).wait_recv()

    def start_pieces(d):
        if d == 0:
            norm = (1.0 / PRESCALE) * float(SEGS * ROWS) ** -0.5
            for a in range(2):
                partner_power(a).wait_recv()
                row_scale[a] = jnp.transpose(jnp.broadcast_to(channel_scale(a) * norm, (TILE, TILE)))
        else:
            partner_power(d + 1).wait_recv()
        for a in range(2):
            outside = jnp.logical_and(2 * z + d + a >= 8, b == BLOCKS - 1)
            both = row_scale[a] * (channel_scale(d + a) * jnp.where(outside, 0.0, 1.0))
            partner_terms(d, a).wait_recv()
            for q in range(4):
                total = acc[d, a, 2 * q + yl] + recv_y[d, a, q].astype(jnp.float32)
                send_z[d, q, a] = (total * both).astype(jnp.bfloat16)
        for k in (2, 1, 3):
            piece_copy(d, k).start()
        piece[d][pl.ds(2 * z, 2)] = send_z[d, z]

    def owner_copy(d, e):
        o = (b + e) % BLOCKS
        return remote(send_o.at[d, e], recv_o[d].at[b], o_send.at[d, e], o_recv.at[d, b], dev(o, t))

    def wait_owner(d, e):
        s = (b + e) % BLOCKS
        remote(send_o.at[d, e], recv_o[d].at[s], o_send.at[d, e], o_recv.at[d, s], partner).wait_recv()

    def start_owners(d):
        for k in (1, 3, 2):
            wait_piece(d, k)

        def send(e, _):
            send_o[d, e] = piece[d][pos_ref[(b + e) % BLOCKS]]
            owner_copy(d, e).start()
            return 0

        lax.fori_loop(1, BLOCKS, send, 0)
        recv_o[d][b] = piece[d][pos_ref[b]]

    def slot_dst(d, lag):
        return out_ref.at[:, lag, :, pl.ds(d * TILE, TILE)]

    def slot_copy(d, e):
        return remote(
            send_t.at[d, e], slot_dst(d, t), t_send.at[d, e], t_recv.at[d, t],
            dev(b, (t + e) % SEGS),
        )

    def own_slots(d):
        return pltpu.make_async_copy(send_t.at[d, 0], slot_dst(d, t), t_recv.at[d, t])

    def wait_slots(d, e):
        s = (t + e) % SEGS
        remote(send_t.at[d, e], slot_dst(d, s), t_send.at[d, e], t_recv.at[d, s], partner).wait_recv()

    def start_slots(d):
        def arrive(e, _):
            wait_owner(d, e)
            return 0

        lax.fori_loop(1, BLOCKS, arrive, 0)

        def fill(e):
            base = 2 * ((t + e) % SEGS)
            for i in range(2):
                taken = recv_o[d][src_ref[base + i]]
                keep = jnp.broadcast_to(fill_ref[base + i], (TILE, TILE)) > 0
                send_t[d, e, i] = jnp.where(keep, taken.astype(jnp.float32), 0.0).astype(jnp.bfloat16)

        def send(e, _):
            fill(e)
            slot_copy(d, e).start()
            return 0

        lax.fori_loop(1, SEGS, send, 0)
        fill(0)
        own_slots(d).start()

    compute(0)
    compute(1)
    start_pieces(0)
    compute(2)
    start_owners(0)
    start_pieces(1)
    compute(3)
    start_slots(0)
    start_owners(1)
    start_pieces(2)
    compute(4)
    start_slots(1)
    start_owners(2)
    start_pieces(3)
    start_slots(2)
    start_owners(3)
    start_slots(3)

    for k in range(4):
        halo_copy(k).wait_send()
    for i in range(APER):
        following_copy(i).wait_send()
    for c in range(5):
        for k in (1, 2, 3):
            if k == 2 and c in FORWARDS:
                forward(c).wait_send()
            else:
                window_copy(k, c, own_tile(c)).wait_send()
        partner_power(c).wait_send()
    for d in range(4):
        for a in range(2):
            partner_terms(d, a).wait_send()
        for k in (1, 2, 3):
            piece_copy(d, k).wait_send()

        def owner_done(e, _, d=d):
            owner_copy(d, e).wait_send()
            return 0

        lax.fori_loop(1, BLOCKS, owner_done, 0)

        def slot_done(e, _, d=d):
            slot_copy(d, e).wait_send()
            wait_slots(d, e)
            return 0

        lax.fori_loop(1, SEGS, slot_done, 0)
        own_slots(d).wait()


def route(tile_owner):
    owner_table = tile_owner.reshape(BLOCKS, NT_HERE)
    my_index = lax.axis_index(("rowblk", "colblk"))
    my_owners = lax.dynamic_index_in_dim(owner_table, my_index, 0, keepdims=False)
    targets = jnp.arange(BLOCKS, dtype=jnp.int32)
    matches = my_owners[None, :] == targets[:, None]
    local_pos = jnp.sum(
        jnp.where(matches, jnp.arange(NT_HERE, dtype=jnp.int32)[None, :], 0), axis=1
    )
    arrived = jnp.any(owner_table == my_index, axis=1)
    slot_rank = jnp.cumsum(arrived.astype(jnp.int32)) - 1
    picker = (slot_rank[None, :] == jnp.arange(OCAP, dtype=jnp.int32)[:, None]) & arrived[None, :]
    source_of = jnp.sum(jnp.where(picker, targets[None, :], 0), axis=1)
    filled = jnp.any(picker, axis=1).astype(jnp.int32)
    return local_pos, source_of, filled


NT_HERE = 8


def shards(signal, tile_owner):
    local_pos, source_of, filled = route(tile_owner)
    bf16, f32, vmem, dma = jnp.bfloat16, jnp.float32, pltpu.VMEM, pltpu.SemaphoreType.DMA
    out = pl.pallas_call(
        kernel,
        out_shape=jax.ShapeDtypeStruct((2, LAGS, TILE, WIN), bf16),
        in_specs=[pl.BlockSpec(memory_space=pltpu.SMEM)] * 3 + [pl.BlockSpec(memory_space=pl.ANY)],
        out_specs=pl.BlockSpec(memory_space=pl.ANY),
        scratch_shapes=[
            vmem((4, ROWS, 5 * TILE), bf16),
            vmem((4, HALO, HALF), bf16),
            vmem((APER, ROWS, TILE), bf16),
            vmem((4, 2, LAGS * TILE, ROWS), bf16),
            vmem((4, 2, LAGS, TILE, TILE), f32),
            vmem((5, 8, TILE), f32),
            vmem((5, 8, TILE), f32),
            vmem((2, TILE, TILE), f32),
            vmem((4, 2, 4, TILE, TILE), bf16),
            vmem((4, 2, 4, TILE, TILE), bf16),
            vmem((4, 4, 2, TILE, TILE), bf16),
        ]
        + [vmem((8, TILE, TILE), bf16)] * 4
        + [vmem((BLOCKS, TILE, TILE), bf16)] * 4
        + [
            vmem((4, BLOCKS, TILE, TILE), bf16),
            vmem((4, SEGS, 2, TILE, TILE), bf16),
            dma((4, 5)), dma((4, 5)), dma((4,)), dma((3,)), dma((3,)), dma((4,)), dma((4,)), dma((5,)), dma((5,)), dma((4, 2)), dma((4, 2)),
            dma((4, 4)), dma((4, 4)), dma((4, BLOCKS)), dma((4, BLOCKS)), dma((4, SEGS)), dma((4, SEGS)),
        ],
        compiler_params=pltpu.CompilerParams(
            collective_id=0, has_side_effects=True, vmem_limit_bytes=48 * 1024 * 1024
        ),
    )(local_pos, source_of, filled, signal)
    return out.astype(f32)[None]


def solution(mesh):
    return jax.shard_map(
        shards,
        mesh=mesh,
        in_specs=(P("tm", ("rowblk", "colblk")), P()),
        out_specs=P(("rowblk", "colblk"), "tm", None, None, None),
        check_vma=False,
    )
```

```python
import functools

import jax
import jax.numpy as jnp
from jax import lax
from jax.experimental import pallas as pl
from jax.experimental.pallas import tpu as pltpu
from jax.sharding import PartitionSpec as P

MESH = pl.DeviceIdType.MESH
TILE = 128
LAGS = 8
APER = 3
OCAP = 16
BLOCKS = 16
SEGS = 8
ROWS = 768
WIN = 512
HALF = 256
HALO = 16
PRESCALE = 2.0**40
FORWARDS = ()
FIRST_SENDS = ((2, 0), (1, 0), (3, 0), (2, 1), (1, 1), (3, 1))
LATER_SENDS = (
    ((2, 2), (1, 2), (3, 2), (0, 2)), ((2, 3), (1, 3), (3, 3), (0, 3)), ((2, 4), (1, 4), (3, 4), (0, 4)), (), (),
)


def kernel(
    pos_ref, src_ref, fill_ref, sig_ref, out_ref,
    ybuf, halo, following, amat, acc, pow_mine, pow_other, row_scale, send_y, recv_y, send_z,
    piece_0, piece_1, piece_2, piece_3, recv_o_0, recv_o_1, recv_o_2, recv_o_3, send_o, send_t,
    g_send, g_recv, f_send, n_send, n_recv, h_send, h_recv, p_send, p_recv, y_send, y_recv,
    z_send, z_recv, o_send, o_recv, t_send, t_recv,
):
    t = lax.axis_index("tm")
    row = lax.axis_index("rowblk")
    col = lax.axis_index("colblk")
    b = row * 4 + col
    z = t // 2
    yl = t % 2
    piece = (piece_0, piece_1, piece_2, piece_3)
    recv_o = (recv_o_0, recv_o_1, recv_o_2, recv_o_3)

    def dev(block, tm):
        return (tm, block // 4, block % 4)

    def remote(src, dst, send_sem, recv_sem, device):
        return pltpu.make_async_remote_copy(
            src_ref=src, dst_ref=dst, send_sem=send_sem, recv_sem=recv_sem,
            device_id=device, device_id_type=MESH,
        )

    partner = dev(b, 2 * z + 1 - yl)

    barrier = pltpu.get_barrier_semaphore()
    for d in range(1, SEGS):
        pl.semaphore_signal(barrier, inc=1, device_id=dev(b, (t + d) % SEGS), device_id_type=MESH)
    for d, k in ((1, 2), (BLOCKS - 1, SEGS - 2)):
        pl.semaphore_signal(
            barrier, inc=1, device_id=dev((b + d) % BLOCKS, (t + k) % SEGS), device_id_type=MESH
        )
    for d in range(1, BLOCKS):
        pl.semaphore_signal(barrier, inc=1, device_id=dev((b + d) % BLOCKS, t), device_id_type=MESH)

    def window_dst(c):
        return ybuf.at[z, :, pl.ds(c * TILE, TILE)]

    def own_tile(g):
        return sig_ref.at[:, pl.ds(pl.multiple_of(g * TILE, TILE), TILE)]

    def window_copy(k, c, src):
        zd = (z + k) % 4
        return remote(src, window_dst(c), g_send.at[k, c], g_recv.at[z, c], dev(b, 2 * zd + yl))

    def start_window(k, c):
        g = 2 * ((z + k) % 4) + c

        def start(src):
            if k == 0:
                pltpu.make_async_copy(src, window_dst(c), g_recv.at[z, c]).start()
            else:
                window_copy(k, c, src).start()

        if c < 2:
            start(own_tile(g))
        else:
            pl.when(g < 8)(lambda: start(own_tile(g)))
            pl.when(g >= 8)(lambda: start(following.at[g - 8]))

    def wait_window(k, c):
        s = (z + k) % 4
        dst = ybuf.at[s, :, pl.ds(c * TILE, TILE)]
        if k == 0:
            pltpu.make_async_copy(dst, dst, g_recv.at[s, c]).wait()
        else:
            remote(dst, dst, g_send.at[k, c], g_recv.at[s, c], partner).wait_recv()

    def following_copy(i):
        return remote(
            own_tile(i), following.at[i], n_send.at[i], n_recv.at[i], dev((b + BLOCKS - 1) % BLOCKS, t)
        )

    def forward(c):
        step, held = (1, 3) if c == 1 else (3, c - 2)
        s = (z + 3) % 4 if c == 1 else (z + 1) % 4
        zd = (z + step) % 4
        block = (b + (z + step) // 4 + (BLOCKS if c == 1 else BLOCKS - 1)) % BLOCKS
        return remote(
            ybuf.at[s, :, pl.ds(held * TILE, TILE)], ybuf.at[s, :, pl.ds(c * TILE, TILE)],
            f_send.at[c - 1], g_recv.at[s, c], dev(block, 2 * zd + yl),
        )

    def halo_copy(k):
        zd = (z + k) % 4
        slot = (z + yl) % 4
        src = sig_ref.at[pl.ds(ROWS - HALO, HALO), pl.ds(pl.multiple_of(zd * HALF, HALF), HALF)]
        return remote(src, halo.at[slot], h_send.at[k], h_recv.at[slot], dev(b, 2 * zd + 1 - yl))

    def wait_halo(s):
        remote(halo.at[s], halo.at[s], h_send.at[0], h_recv.at[s], partner).wait_recv()

    for c in range(2):
        start_window(0, c)

    pl.semaphore_wait(barrier, SEGS - 1 + BLOCKS - 1 + 2)

    for k in range(4):
        halo_copy(k).start()
    for i in range(APER):
        following_copy(i).start()
    for k, c in FIRST_SENDS:
        start_window(k, c)

    def square_sums(s, c, first):
        v = ybuf[s, :, c * TILE : (c + 1) * TILE].astype(jnp.float32)
        total = jnp.sum((v * v).reshape(ROWS // 8, 8, TILE), axis=0)
        pow_mine[c] = total if first else pow_mine[c] + total

    def build_lags(s, a):
        keep = jnp.where(jnp.logical_and(s == 0, yl == 0), 0.0, PRESCALE)
        x = ybuf[s, :, a * TILE : (a + 1) * TILE].astype(jnp.float32) * PRESCALE
        h = halo[s, :, a * TILE : (a + 1) * TILE].astype(jnp.float32) * keep
        rows = jnp.concatenate([jnp.zeros((TILE - HALO, TILE), jnp.float32), h, x], axis=0)
        cols = jnp.transpose(rows)
        for j in range(LAGS):
            shifted = cols if j == 0 else pltpu.roll(cols, j, 1)
            amat[s, a, j * TILE : (j + 1) * TILE, :] = shifted[:, TILE:].astype(jnp.bfloat16)

    def products(s, c, first):
        y = ybuf[s, :, c * TILE : (c + 1) * TILE]
        for a in range(2):
            d = c - a
            if 0 <= d < 4:
                for j in range(0, LAGS, 4):
                    p = jnp.dot(
                        amat[s, a, j * TILE : (j + 4) * TILE, :], y, preferred_element_type=jnp.float32
                    ).reshape(4, TILE, TILE)
                    acc[d, a, j : j + 4] = p if first else acc[d, a, j : j + 4] + p

    def partner_power(c):
        return remote(pow_mine.at[c], pow_other.at[c], p_send.at[c], p_recv.at[c], partner)

    def partner_terms(d, a):
        return remote(send_y.at[d, a], recv_y.at[d, a], y_send.at[d, a], y_recv.at[d, a], partner)

    def compute(c):
        for k in (0, 1, 3, 2):
            s = (z + k) % 4
            if c == 0:
                wait_halo(s)
            if c == 1 and k == 2 and 1 in FORWARDS:
                wait_window(3, 3)
                forward(1).start()
            if not (k == 3 and c == 3 and 1 in FORWARDS):
                wait_window(k, c)
            if k == 1 and c + 2 in FORWARDS:
                forward(c + 2).start()
            if c < 2:
                build_lags(s, c)
            products(s, c, k == 0)
            square_sums(s, c, k == 0)
        if c == 0:
            for i in range(APER):
                following_copy(i).wait_recv()
        for k, e in LATER_SENDS[c]:
            start_window(k, e)
        partner_power(c).start()
        for a in range(2):
            d = c - a
            if 0 <= d < 4:
                for q in range(4):
                    send_y[d, a, q] = acc[d, a, 2 * q + 1 - yl].astype(jnp.bfloat16)
                partner_terms(d, a).start()

    def channel_scale(c):
        total = jnp.sum(pow_mine[c] + pow_other[c], axis=0, keepdims=True)
        return lax.rsqrt(total * (1.0 / (SEGS * ROWS)) + 1e-06)

    def piece_copy(d, k):
        zd = (z + k) % 4
        return remote(
            send_z.at[d, zd], piece[d].at[pl.ds(2 * z, 2)], z_send.at[d, k], z_recv.at[d, z],
            dev(b, 2 * zd + yl),
        )

    def wait_piece(d, k):
        s = (z + k) % 4
        remote(
            send_z.at[d, s], piece[d].at[pl.ds(2 * s, 2)], z_send.at[d, k], z_recv.at[d, s], partner
        ).wait_recv()

    def start_pieces(d):
        if d == 0:
            norm = (1.0 / PRESCALE) * float(SEGS * ROWS) ** -0.5
            for a in range(2):
                partner_power(a).wait_recv()
                row_scale[a] = jnp.transpose(jnp.broadcast_to(channel_scale(a) * norm, (TILE, TILE)))
        else:
            partner_power(d + 1).wait_recv()
        for a in range(2):
            outside = jnp.logical_and(2 * z + d + a >= 8, b == BLOCKS - 1)
            both = row_scale[a] * (channel_scale(d + a) * jnp.where(outside, 0.0, 1.0))
            partner_terms(d, a).wait_recv()
            for q in range(4):
                total = acc[d, a, 2 * q + yl] + recv_y[d, a, q].astype(jnp.float32)
                send_z[d, q, a] = (total * both).astype(jnp.bfloat16)
        for k in (2, 1, 3):
            piece_copy(d, k).start()
        piece[d][pl.ds(2 * z, 2)] = send_z[d, z]

    def owner_copy(d, e):
        o = (b + e) % BLOCKS
        return remote(send_o.at[d, e], recv_o[d].at[b], o_send.at[d, e], o_recv.at[d, b], dev(o, t))

    def wait_owner(d, e):
        s = (b + e) % BLOCKS
        remote(send_o.at[d, e], recv_o[d].at[s], o_send.at[d, e], o_recv.at[d, s], partner).wait_recv()

    def start_owners(d):
        for k in (1, 3, 2):
            wait_piece(d, k)

        def send(e, _):
            send_o[d, e] = piece[d][pos_ref[(b + e) % BLOCKS]]
            owner_copy(d, e).start()
            return 0

        lax.fori_loop(1, BLOCKS, send, 0)
        recv_o[d][b] = piece[d][pos_ref[b]]

    def slot_dst(d, lag):
        return out_ref.at[:, lag, :, pl.ds(d * TILE, TILE)]

    def slot_copy(d, e):
        return remote(
            send_t.at[d, e], slot_dst(d, t), t_send.at[d, e], t_recv.at[d, t],
            dev(b, (t + e) % SEGS),
        )

    def own_slots(d):
        return pltpu.make_async_copy(send_t.at[d, 0], slot_dst(d, t), t_recv.at[d, t])

    def wait_slots(d, e):
        s = (t + e) % SEGS
        remote(send_t.at[d, e], slot_dst(d, s), t_send.at[d, e], t_recv.at[d, s], partner).wait_recv()

    def start_slots(d):
        def arrive(e, _):
            wait_owner(d, e)
            return 0

        lax.fori_loop(1, BLOCKS, arrive, 0)

        def fill(e):
            base = 2 * ((t + e) % SEGS)
            for i in range(2):
                taken = recv_o[d][src_ref[base + i]]
                keep = jnp.broadcast_to(fill_ref[base + i], (TILE, TILE)) > 0
                send_t[d, e, i] = jnp.where(keep, taken.astype(jnp.float32), 0.0).astype(jnp.bfloat16)

        def send(e, _):
            fill(e)
            slot_copy(d, e).start()
            return 0

        lax.fori_loop(1, SEGS, send, 0)
        fill(0)
        own_slots(d).start()

    compute(0)
    compute(1)
    start_pieces(0)
    compute(2)
    start_pieces(1)
    start_owners(0)
    compute(3)
    start_pieces(2)
    start_owners(1)
    compute(4)
    start_pieces(3)
    start_owners(2)
    start_slots(0)
    start_owners(3)
    start_slots(1)
    start_slots(2)
    start_slots(3)

    for k in range(4):
        halo_copy(k).wait_send()
    for i in range(APER):
        following_copy(i).wait_send()
    for c in range(5):
        for k in (1, 2, 3):
            if k == 2 and c in FORWARDS:
                forward(c).wait_send()
            else:
                window_copy(k, c, own_tile(c)).wait_send()
        partner_power(c).wait_send()
    for d in range(4):
        for a in range(2):
            partner_terms(d, a).wait_send()
        for k in (1, 2, 3):
            piece_copy(d, k).wait_send()

        def owner_done(e, _, d=d):
            owner_copy(d, e).wait_send()
            return 0

        lax.fori_loop(1, BLOCKS, owner_done, 0)

        def slot_done(e, _, d=d):
            slot_copy(d, e).wait_send()
            wait_slots(d, e)
            return 0

        lax.fori_loop(1, SEGS, slot_done, 0)
        own_slots(d).wait()


def route(tile_owner):
    owner_table = tile_owner.reshape(BLOCKS, NT_HERE)
    my_index = lax.axis_index(("rowblk", "colblk"))
    my_owners = lax.dynamic_index_in_dim(owner_table, my_index, 0, keepdims=False)
    targets = jnp.arange(BLOCKS, dtype=jnp.int32)
    matches = my_owners[None, :] == targets[:, None]
    local_pos = jnp.sum(
        jnp.where(matches, jnp.arange(NT_HERE, dtype=jnp.int32)[None, :], 0), axis=1
    )
    arrived = jnp.any(owner_table == my_index, axis=1)
    slot_rank = jnp.cumsum(arrived.astype(jnp.int32)) - 1
    picker = (slot_rank[None, :] == jnp.arange(OCAP, dtype=jnp.int32)[:, None]) & arrived[None, :]
    source_of = jnp.sum(jnp.where(picker, targets[None, :], 0), axis=1)
    filled = jnp.any(picker, axis=1).astype(jnp.int32)
    return local_pos, source_of, filled


NT_HERE = 8


def shards(signal, tile_owner):
    local_pos, source_of, filled = route(tile_owner)
    bf16, f32, vmem, dma = jnp.bfloat16, jnp.float32, pltpu.VMEM, pltpu.SemaphoreType.DMA
    out = pl.pallas_call(
        kernel,
        out_shape=jax.ShapeDtypeStruct((2, LAGS, TILE, WIN), bf16),
        in_specs=[pl.BlockSpec(memory_space=pltpu.SMEM)] * 3 + [pl.BlockSpec(memory_space=pl.ANY)],
        out_specs=pl.BlockSpec(memory_space=pl.ANY),
        scratch_shapes=[
            vmem((4, ROWS, 5 * TILE), bf16),
            vmem((4, HALO, HALF), bf16),
            vmem((APER, ROWS, TILE), bf16),
            vmem((4, 2, LAGS * TILE, ROWS), bf16),
            vmem((4, 2, LAGS, TILE, TILE), f32),
            vmem((5, 8, TILE), f32),
            vmem((5, 8, TILE), f32),
            vmem((2, TILE, TILE), f32),
            vmem((4, 2, 4, TILE, TILE), bf16),
            vmem((4, 2, 4, TILE, TILE), bf16),
            vmem((4, 4, 2, TILE, TILE), bf16),
        ]
        + [vmem((8, TILE, TILE), bf16)] * 4
        + [vmem((BLOCKS, TILE, TILE), bf16)] * 4
        + [
            vmem((4, BLOCKS, TILE, TILE), bf16),
            vmem((4, SEGS, 2, TILE, TILE), bf16),
            dma((4, 5)), dma((4, 5)), dma((4,)), dma((3,)), dma((3,)), dma((4,)), dma((4,)), dma((5,)), dma((5,)), dma((4, 2)), dma((4, 2)),
            dma((4, 4)), dma((4, 4)), dma((4, BLOCKS)), dma((4, BLOCKS)), dma((4, SEGS)), dma((4, SEGS)),
        ],
        compiler_params=pltpu.CompilerParams(
            collective_id=0, has_side_effects=True, vmem_limit_bytes=48 * 1024 * 1024
        ),
    )(local_pos, source_of, filled, signal)
    return out.astype(f32)[None]


def solution(mesh):
    return jax.shard_map(
        shards,
        mesh=mesh,
        in_specs=(P("tm", ("rowblk", "colblk")), P()),
        out_specs=P(("rowblk", "colblk"), "tm", None, None, None),
        check_vma=False,
    )
```

```python
import functools

import jax
import jax.numpy as jnp
from jax import lax
from jax.experimental import pallas as pl
from jax.experimental.pallas import tpu as pltpu
from jax.sharding import PartitionSpec as P

MESH = pl.DeviceIdType.MESH
TILE = 128
LAGS = 8
APER = 3
OCAP = 16
BLOCKS = 16
SEGS = 8
ROWS = 768
WIN = 512
HALF = 256
HALO = 16
PRESCALE = 2.0**40
FIRST_SENDS = ((2, 0), (1, 0), (3, 0), (2, 1), (1, 1), (3, 1))
LATER_SENDS = (
    ((2, 2), (1, 2), (3, 2), (0, 2)), ((2, 3), (1, 3), (3, 3), (0, 3)), ((2, 4), (1, 4), (3, 4), (0, 4)), (), (),
)


def kernel(
    pos_ref, src_ref, fill_ref, sig_ref, out_ref,
    ybuf, halo, following, amat, acc, pow_mine, pow_other, row_scale, send_y, recv_y, send_z,
    piece_0, piece_1, piece_2, piece_3, recv_o_0, recv_o_1, recv_o_2, recv_o_3, send_o, send_t,
    g_send, g_recv, n_send, n_recv, h_send, h_recv, p_send, p_recv, y_send, y_recv,
    z_send, z_recv, o_send, o_recv, t_send, t_recv,
):
    t = lax.axis_index("tm")
    row = lax.axis_index("rowblk")
    col = lax.axis_index("colblk")
    b = row * 4 + col
    z = t // 2
    yl = t % 2
    piece = (piece_0, piece_1, piece_2, piece_3)
    recv_o = (recv_o_0, recv_o_1, recv_o_2, recv_o_3)

    def dev(block, tm):
        return (tm, block // 4, block % 4)

    def remote(src, dst, send_sem, recv_sem, device):
        return pltpu.make_async_remote_copy(
            src_ref=src, dst_ref=dst, send_sem=send_sem, recv_sem=recv_sem,
            device_id=device, device_id_type=MESH,
        )

    partner = dev(b, 2 * z + 1 - yl)

    barrier = pltpu.get_barrier_semaphore()
    for d in range(1, SEGS):
        pl.semaphore_signal(barrier, inc=1, device_id=dev(b, (t + d) % SEGS), device_id_type=MESH)
    for d in range(1, BLOCKS):
        pl.semaphore_signal(barrier, inc=1, device_id=dev((b + d) % BLOCKS, t), device_id_type=MESH)

    def window_dst(c):
        return ybuf.at[z, :, pl.ds(c * TILE, TILE)]

    def own_tile(g):
        return sig_ref.at[:, pl.ds(pl.multiple_of(g * TILE, TILE), TILE)]

    def window_copy(k, c, src):
        zd = (z + k) % 4
        return remote(src, window_dst(c), g_send.at[k, c], g_recv.at[z, c], dev(b, 2 * zd + yl))

    def start_window(k, c):
        g = 2 * ((z + k) % 4) + c

        def start(src):
            if k == 0:
                pltpu.make_async_copy(src, window_dst(c), g_recv.at[z, c]).start()
            else:
                window_copy(k, c, src).start()

        if c < 2:
            start(own_tile(g))
        else:
            pl.when(g < 8)(lambda: start(own_tile(g)))
            pl.when(g >= 8)(lambda: start(following.at[g - 8]))

    def wait_window(k, c):
        s = (z + k) % 4
        dst = ybuf.at[s, :, pl.ds(c * TILE, TILE)]
        if k == 0:
            pltpu.make_async_copy(dst, dst, g_recv.at[s, c]).wait()
        else:
            remote(dst, dst, g_send.at[k, c], g_recv.at[s, c], partner).wait_recv()

    def following_copy(i):
        return remote(
            own_tile(i), following.at[i], n_send.at[i], n_recv.at[i], dev((b + BLOCKS - 1) % BLOCKS, t)
        )

    def halo_copy(k):
        zd = (z + k) % 4
        slot = (z + yl) % 4
        src = sig_ref.at[pl.ds(ROWS - HALO, HALO), pl.ds(pl.multiple_of(zd * HALF, HALF), HALF)]
        return remote(src, halo.at[slot], h_send.at[k], h_recv.at[slot], dev(b, 2 * zd + 1 - yl))

    def wait_halo(s):
        remote(halo.at[s], halo.at[s], h_send.at[0], h_recv.at[s], partner).wait_recv()

    for c in range(2):
        start_window(0, c)

    pl.semaphore_wait(barrier, SEGS - 1 + BLOCKS - 1)

    for k in range(4):
        halo_copy(k).start()
    for i in range(APER):
        following_copy(i).start()
    for k, c in FIRST_SENDS:
        start_window(k, c)

    def square_sums(s, c, first):
        v = ybuf[s, :, c * TILE : (c + 1) * TILE].astype(jnp.float32)
        total = jnp.sum((v * v).reshape(ROWS // 8, 8, TILE), axis=0)
        pow_mine[c] = total if first else pow_mine[c] + total

    def build_lags(s, a):
        keep = jnp.where(jnp.logical_and(s == 0, yl == 0), 0.0, PRESCALE)
        x = ybuf[s, :, a * TILE : (a + 1) * TILE].astype(jnp.float32) * PRESCALE
        h = halo[s, :, a * TILE : (a + 1) * TILE].astype(jnp.float32) * keep
        rows = jnp.concatenate([jnp.zeros((TILE - HALO, TILE), jnp.float32), h, x], axis=0)
        cols = jnp.transpose(rows)
        for j in range(LAGS):
            shifted = cols if j == 0 else pltpu.roll(cols, j, 1)
            amat[s, a, j * TILE : (j + 1) * TILE, :] = shifted[:, TILE:].astype(jnp.bfloat16)

    def products(s, c, first):
        y = ybuf[s, :, c * TILE : (c + 1) * TILE]
        for a in range(2):
            d = c - a
            if 0 <= d < 4:
                for j in range(0, LAGS, 4):
                    p = jnp.dot(
                        amat[s, a, j * TILE : (j + 4) * TILE, :], y, preferred_element_type=jnp.float32
                    ).reshape(4, TILE, TILE)
                    acc[d, a, j : j + 4] = p if first else acc[d, a, j : j + 4] + p

    def partner_power(c):
        return remote(pow_mine.at[c], pow_other.at[c], p_send.at[c], p_recv.at[c], partner)

    def partner_terms(d, a):
        return remote(send_y.at[d, a], recv_y.at[d, a], y_send.at[d, a], y_recv.at[d, a], partner)

    def compute(c):
        for k in (0, 1, 3, 2):
            s = (z + k) % 4
            if c == 0:
                wait_halo(s)
            wait_window(k, c)
            if c < 2:
                build_lags(s, c)
            products(s, c, k == 0)
            square_sums(s, c, k == 0)
        if c == 0:
            for i in range(APER):
                following_copy(i).wait_recv()
        for k, e in LATER_SENDS[c]:
            start_window(k, e)
        partner_power(c).start()
        for a in range(2):
            d = c - a
            if 0 <= d < 4:
                for q in range(4):
                    send_y[d, a, q] = acc[d, a, 2 * q + 1 - yl].astype(jnp.bfloat16)
                partner_terms(d, a).start()

    def channel_scale(c):
        total = jnp.sum(pow_mine[c] + pow_other[c], axis=0, keepdims=True)
        return lax.rsqrt(total * (1.0 / (SEGS * ROWS)) + 1e-06)

    def piece_copy(d, k):
        zd = (z + k) % 4
        return remote(
            send_z.at[d, zd], piece[d].at[pl.ds(2 * z, 2)], z_send.at[d, k], z_recv.at[d, z],
            dev(b, 2 * zd + yl),
        )

    def wait_piece(d, k):
        s = (z + k) % 4
        remote(
            send_z.at[d, s], piece[d].at[pl.ds(2 * s, 2)], z_send.at[d, k], z_recv.at[d, s], partner
        ).wait_recv()

    def start_pieces(d):
        if d == 0:
            norm = (1.0 / PRESCALE) * float(SEGS * ROWS) ** -0.5
            for a in range(2):
                partner_power(a).wait_recv()
                row_scale[a] = jnp.transpose(jnp.broadcast_to(channel_scale(a) * norm, (TILE, TILE)))
        else:
            partner_power(d + 1).wait_recv()
        for a in range(2):
            outside = jnp.logical_and(2 * z + d + a >= 8, b == BLOCKS - 1)
            both = row_scale[a] * (channel_scale(d + a) * jnp.where(outside, 0.0, 1.0))
            partner_terms(d, a).wait_recv()
            for q in range(4):
                total = acc[d, a, 2 * q + yl] + recv_y[d, a, q].astype(jnp.float32)
                send_z[d, q, a] = (total * both).astype(jnp.bfloat16)
        for k in (2, 1, 3):
            piece_copy(d, k).start()
        piece[d][pl.ds(2 * z, 2)] = send_z[d, z]

    def owner_copy(d, e):
        o = (b + e) % BLOCKS
        return remote(send_o.at[d, e], recv_o[d].at[b], o_send.at[d, e], o_recv.at[d, b], dev(o, t))

    def wait_owner(d, e):
        s = (b + e) % BLOCKS
        remote(send_o.at[d, e], recv_o[d].at[s], o_send.at[d, e], o_recv.at[d, s], partner).wait_recv()

    def start_owners(d):
        for k in (1, 3, 2):
            wait_piece(d, k)

        def send(i, _):
            e = (i * 7) % BLOCKS
            send_o[d, e] = piece[d][pos_ref[(b + e) % BLOCKS]]
            owner_copy(d, e).start()
            return 0

        lax.fori_loop(1, BLOCKS, send, 0)
        recv_o[d][b] = piece[d][pos_ref[b]]

    def slot_dst(d, lag):
        return out_ref.at[:, lag, :, pl.ds(d * TILE, TILE)]

    def slot_copy(d, e):
        return remote(
            send_t.at[d, e], slot_dst(d, t), t_send.at[d, e], t_recv.at[d, t],
            dev(b, (t + e) % SEGS),
        )

    def own_slots(d):
        return pltpu.make_async_copy(send_t.at[d, 0], slot_dst(d, t), t_recv.at[d, t])

    def wait_slots(d, e):
        s = (t + e) % SEGS
        remote(send_t.at[d, e], slot_dst(d, s), t_send.at[d, e], t_recv.at[d, s], partner).wait_recv()

    def start_slots(d):
        def arrive(e, _):
            wait_owner(d, e)
            return 0

        lax.fori_loop(1, BLOCKS, arrive, 0)

        def fill(e):
            base = 2 * ((t + e) % SEGS)
            for i in range(2):
                taken = recv_o[d][src_ref[base + i]]
                keep = jnp.broadcast_to(fill_ref[base + i], (TILE, TILE)) > 0
                send_t[d, e, i] = jnp.where(keep, taken.astype(jnp.float32), 0.0).astype(jnp.bfloat16)

        def send(e, _):
            fill(e)
            slot_copy(d, e).start()
            return 0

        lax.fori_loop(1, SEGS, send, 0)
        fill(0)
        own_slots(d).start()

    compute(0)
    compute(1)
    start_pieces(0)
    compute(2)
    start_owners(0)
    start_pieces(1)
    compute(3)
    start_owners(1)
    start_pieces(2)
    start_slots(0)
    compute(4)
    start_owners(2)
    start_pieces(3)
    start_slots(1)
    start_owners(3)
    start_slots(2)
    start_slots(3)

    for k in range(4):
        halo_copy(k).wait_send()
    for i in range(APER):
        following_copy(i).wait_send()
    for c in range(5):
        for k in (1, 2, 3):
            window_copy(k, c, own_tile(c)).wait_send()
        partner_power(c).wait_send()
    for d in range(4):
        for a in range(2):
            partner_terms(d, a).wait_send()
        for k in (1, 2, 3):
            piece_copy(d, k).wait_send()

        def owner_done(e, _, d=d):
            owner_copy(d, e).wait_send()
            return 0

        lax.fori_loop(1, BLOCKS, owner_done, 0)

        def slot_done(e, _, d=d):
            slot_copy(d, e).wait_send()
            wait_slots(d, e)
            return 0

        lax.fori_loop(1, SEGS, slot_done, 0)
        own_slots(d).wait()


def route(tile_owner):
    owner_table = tile_owner.reshape(BLOCKS, NT_HERE)
    my_index = lax.axis_index(("rowblk", "colblk"))
    my_owners = lax.dynamic_index_in_dim(owner_table, my_index, 0, keepdims=False)
    targets = jnp.arange(BLOCKS, dtype=jnp.int32)
    matches = my_owners[None, :] == targets[:, None]
    local_pos = jnp.sum(
        jnp.where(matches, jnp.arange(NT_HERE, dtype=jnp.int32)[None, :], 0), axis=1
    )
    arrived = jnp.any(owner_table == my_index, axis=1)
    slot_rank = jnp.cumsum(arrived.astype(jnp.int32)) - 1
    picker = (slot_rank[None, :] == jnp.arange(OCAP, dtype=jnp.int32)[:, None]) & arrived[None, :]
    source_of = jnp.sum(jnp.where(picker, targets[None, :], 0), axis=1)
    filled = jnp.any(picker, axis=1).astype(jnp.int32)
    return local_pos, source_of, filled


NT_HERE = 8


def shards(signal, tile_owner):
    local_pos, source_of, filled = route(tile_owner)
    bf16, f32, vmem, dma = jnp.bfloat16, jnp.float32, pltpu.VMEM, pltpu.SemaphoreType.DMA
    out = pl.pallas_call(
        kernel,
        out_shape=jax.ShapeDtypeStruct((2, LAGS, TILE, WIN), bf16),
        in_specs=[pl.BlockSpec(memory_space=pltpu.SMEM)] * 3 + [pl.BlockSpec(memory_space=pl.ANY)],
        out_specs=pl.BlockSpec(memory_space=pl.ANY),
        scratch_shapes=[
            vmem((4, ROWS, 5 * TILE), bf16),
            vmem((4, HALO, HALF), bf16),
            vmem((APER, ROWS, TILE), bf16),
            vmem((4, 2, LAGS * TILE, ROWS), bf16),
            vmem((4, 2, LAGS, TILE, TILE), f32),
            vmem((5, 8, TILE), f32),
            vmem((5, 8, TILE), f32),
            vmem((2, TILE, TILE), f32),
            vmem((4, 2, 4, TILE, TILE), bf16),
            vmem((4, 2, 4, TILE, TILE), bf16),
            vmem((4, 4, 2, TILE, TILE), bf16),
        ]
        + [vmem((8, TILE, TILE), bf16)] * 4
        + [vmem((BLOCKS, TILE, TILE), bf16)] * 4
        + [
            vmem((4, BLOCKS, TILE, TILE), bf16),
            vmem((4, SEGS, 2, TILE, TILE), bf16),
            dma((4, 5)), dma((4, 5)), dma((3,)), dma((3,)), dma((4,)), dma((4,)), dma((5,)), dma((5,)), dma((4, 2)), dma((4, 2)),
            dma((4, 4)), dma((4, 4)), dma((4, BLOCKS)), dma((4, BLOCKS)), dma((4, SEGS)), dma((4, SEGS)),
        ],
        compiler_params=pltpu.CompilerParams(
            collective_id=0, has_side_effects=True, vmem_limit_bytes=48 * 1024 * 1024
        ),
    )(local_pos, source_of, filled, signal)
    return out.astype(f32)[None]


def solution(mesh):
    return jax.shard_map(
        shards,
        mesh=mesh,
        in_specs=(P("tm", ("rowblk", "colblk")), P()),
        out_specs=P(("rowblk", "colblk"), "tm", None, None, None),
        check_vma=False,
    )
```

```python
import functools

import jax
import jax.numpy as jnp
from jax import lax
from jax.experimental import pallas as pl
from jax.experimental.pallas import tpu as pltpu
from jax.sharding import PartitionSpec as P

MESH = pl.DeviceIdType.MESH
TILE = 128
LAGS = 8
APER = 3
OCAP = 16
BLOCKS = 16
SEGS = 8
ROWS = 768
WIN = 512
HALF = 256
HALO = 16
PRESCALE = 2.0**40
FIRST_SENDS = ((2, 0), (1, 0), (3, 0), (2, 1), (1, 1), (3, 1))
LATER_SENDS = (
    ((2, 2), (1, 2), (3, 2), (0, 2)), ((2, 3), (1, 3), (3, 3), (0, 3)), ((2, 4), (1, 4), (3, 4), (0, 4)), (), (),
)


def kernel(
    pos_ref, src_ref, fill_ref, sig_ref, out_ref,
    ybuf, halo, following, amat, acc, pow_mine, pow_other, row_scale, send_y, recv_y, send_z,
    piece_0, piece_1, piece_2, piece_3, recv_o_0, recv_o_1, recv_o_2, recv_o_3, send_o, send_t,
    g_send, g_recv, n_send, n_recv, h_send, h_recv, p_send, p_recv, y_send, y_recv,
    z_send, z_recv, o_send, o_recv, t_send, t_recv,
):
    t = lax.axis_index("tm")
    row = lax.axis_index("rowblk")
    col = lax.axis_index("colblk")
    b = row * 4 + col
    z = t // 2
    yl = t % 2
    piece = (piece_0, piece_1, piece_2, piece_3)
    recv_o = (recv_o_0, recv_o_1, recv_o_2, recv_o_3)

    def dev(block, tm):
        return (tm, block // 4, block % 4)

    def remote(src, dst, send_sem, recv_sem, device):
        return pltpu.make_async_remote_copy(
            src_ref=src, dst_ref=dst, send_sem=send_sem, recv_sem=recv_sem,
            device_id=device, device_id_type=MESH,
        )

    partner = dev(b, 2 * z + 1 - yl)

    barrier = pltpu.get_barrier_semaphore()
    for d in range(1, SEGS):
        pl.semaphore_signal(barrier, inc=1, device_id=dev(b, (t + d) % SEGS), device_id_type=MESH)
    for d in range(1, BLOCKS):
        pl.semaphore_signal(barrier, inc=1, device_id=dev((b + d) % BLOCKS, t), device_id_type=MESH)

    def window_dst(c):
        return ybuf.at[z, :, pl.ds(c * TILE, TILE)]

    def own_tile(g):
        return sig_ref.at[:, pl.ds(pl.multiple_of(g * TILE, TILE), TILE)]

    def window_copy(k, c, src):
        zd = (z + k) % 4
        return remote(src, window_dst(c), g_send.at[k, c], g_recv.at[z, c], dev(b, 2 * zd + yl))

    def start_window(k, c):
        g = 2 * ((z + k) % 4) + c

        def start(src):
            if k == 0:
                pltpu.make_async_copy(src, window_dst(c), g_recv.at[z, c]).start()
            else:
                window_copy(k, c, src).start()

        if c < 2:
            start(own_tile(g))
        else:
            pl.when(g < 8)(lambda: start(own_tile(g)))
            pl.when(g >= 8)(lambda: start(following.at[g - 8]))

    def wait_window(k, c):
        s = (z + k) % 4
        dst = ybuf.at[s, :, pl.ds(c * TILE, TILE)]
        if k == 0:
            pltpu.make_async_copy(dst, dst, g_recv.at[s, c]).wait()
        else:
            remote(dst, dst, g_send.at[k, c], g_recv.at[s, c], partner).wait_recv()

    def following_copy(i):
        return remote(
            own_tile(i), following.at[i], n_send.at[i], n_recv.at[i], dev((b + BLOCKS - 1) % BLOCKS, t)
        )

    def halo_copy(k):
        zd = (z + k) % 4
        slot = (z + yl) % 4
        src = sig_ref.at[pl.ds(ROWS - HALO, HALO), pl.ds(pl.multiple_of(zd * HALF, HALF), HALF)]
        return remote(src, halo.at[slot], h_send.at[k], h_recv.at[slot], dev(b, 2 * zd + 1 - yl))

    def wait_halo(s):
        remote(halo.at[s], halo.at[s], h_send.at[0], h_recv.at[s], partner).wait_recv()

    for c in range(2):
        start_window(0, c)

    pl.semaphore_wait(barrier, SEGS - 1 + BLOCKS - 1)

    for k in range(4):
        halo_copy(k).start()
    for i in range(APER):
        following_copy(i).start()
    for k, c in FIRST_SENDS:
        start_window(k, c)

    def square_sums(s, c, first):
        v = ybuf[s, :, c * TILE : (c + 1) * TILE].astype(jnp.float32)
        total = jnp.sum((v * v).reshape(ROWS // 8, 8, TILE), axis=0)
        pow_mine[c] = total if first else pow_mine[c] + total

    def build_lags(s, a):
        keep = jnp.where(jnp.logical_and(s == 0, yl == 0), 0.0, PRESCALE)
        x = ybuf[s, :, a * TILE : (a + 1) * TILE].astype(jnp.float32) * PRESCALE
        h = halo[s, :, a * TILE : (a + 1) * TILE].astype(jnp.float32) * keep
        rows = jnp.concatenate([jnp.zeros((TILE - HALO, TILE), jnp.float32), h, x], axis=0)
        cols = jnp.transpose(rows)
        for j in range(LAGS):
            shifted = cols if j == 0 else pltpu.roll(cols, j, 1)
            amat[s, a, j * TILE : (j + 1) * TILE, :] = shifted[:, TILE:].astype(jnp.bfloat16)

    def products(s, c, first):
        y = ybuf[s, :, c * TILE : (c + 1) * TILE]
        for a in range(2):
            d = c - a
            if 0 <= d < 4:
                for j in range(0, LAGS, 4):
                    p = jnp.dot(
                        amat[s, a, j * TILE : (j + 4) * TILE, :], y, preferred_element_type=jnp.float32
                    ).reshape(4, TILE, TILE)
                    acc[d, a, j : j + 4] = p if first else acc[d, a, j : j + 4] + p

    def partner_power(c):
        return remote(pow_mine.at[c], pow_other.at[c], p_send.at[c], p_recv.at[c], partner)

    def partner_terms(d, a):
        return remote(send_y.at[d, a], recv_y.at[d, a], y_send.at[d, a], y_recv.at[d, a], partner)

    def compute(c):
        for k in (0, 1, 3, 2):
            s = (z + k) % 4
            if c == 0:
                wait_halo(s)
            wait_window(k, c)
            if c < 2:
                build_lags(s, c)
            products(s, c, k == 0)
            square_sums(s, c, k == 0)
        if c == 0:
            for i in range(APER):
                following_copy(i).wait_recv()
        for k, e in LATER_SENDS[c]:
            start_window(k, e)
        partner_power(c).start()
        for a in range(2):
            d = c - a
            if 0 <= d < 4:
                for q in range(4):
                    send_y[d, a, q] = acc[d, a, 2 * q + 1 - yl].astype(jnp.bfloat16)
                partner_terms(d, a).start()

    def channel_scale(c):
        total = jnp.sum(pow_mine[c] + pow_other[c], axis=0, keepdims=True)
        return lax.rsqrt(total * (1.0 / (SEGS * ROWS)) + 1e-06)

    def piece_copy(d, k):
        zd = (z + k) % 4
        return remote(
            send_z.at[d, zd], piece[d].at[pl.ds(2 * z, 2)], z_send.at[d, k], z_recv.at[d, z],
            dev(b, 2 * zd + yl),
        )

    def wait_piece(d, k):
        s = (z + k) % 4
        remote(
            send_z.at[d, s], piece[d].at[pl.ds(2 * s, 2)], z_send.at[d, k], z_recv.at[d, s], partner
        ).wait_recv()

    def start_pieces(d):
        if d == 0:
            norm = (1.0 / PRESCALE) * float(SEGS * ROWS) ** -0.5
            for a in range(2):
                partner_power(a).wait_recv()
                row_scale[a] = jnp.transpose(jnp.broadcast_to(channel_scale(a) * norm, (TILE, TILE)))
        else:
            partner_power(d + 1).wait_recv()
        for a in range(2):
            outside = jnp.logical_and(2 * z + d + a >= 8, b == BLOCKS - 1)
            both = row_scale[a] * (channel_scale(d + a) * jnp.where(outside, 0.0, 1.0))
            partner_terms(d, a).wait_recv()
            for q in range(4):
                total = acc[d, a, 2 * q + yl] + recv_y[d, a, q].astype(jnp.float32)
                send_z[d, q, a] = (total * both).astype(jnp.bfloat16)
        for k in (2, 1, 3):
            piece_copy(d, k).start()
        piece[d][pl.ds(2 * z, 2)] = send_z[d, z]

    def owner_copy(d, e):
        o = (b + e) % BLOCKS
        return remote(send_o.at[d, e], recv_o[d].at[b], o_send.at[d, e], o_recv.at[d, b], dev(o, t))

    def wait_owner(d, e):
        s = (b + e) % BLOCKS
        remote(send_o.at[d, e], recv_o[d].at[s], o_send.at[d, e], o_recv.at[d, s], partner).wait_recv()

    def start_owners(d):
        for k in (1, 3, 2):
            wait_piece(d, k)

        def send(i, _):
            e = (i * 3) % BLOCKS
            send_o[d, e] = piece[d][pos_ref[(b + e) % BLOCKS]]
            owner_copy(d, e).start()
            return 0

        lax.fori_loop(1, BLOCKS, send, 0)
        recv_o[d][b] = piece[d][pos_ref[b]]

    def slot_dst(d, lag):
        return out_ref.at[:, lag, :, pl.ds(d * TILE, TILE)]

    def slot_copy(d, e):
        return remote(
            send_t.at[d, e], slot_dst(d, t), t_send.at[d, e], t_recv.at[d, t],
            dev(b, (t + e) % SEGS),
        )

    def own_slots(d):
        return pltpu.make_async_copy(send_t.at[d, 0], slot_dst(d, t), t_recv.at[d, t])

    def wait_slots(d, e):
        s = (t + e) % SEGS
        remote(send_t.at[d, e], slot_dst(d, s), t_send.at[d, e], t_recv.at[d, s], partner).wait_recv()

    def start_slots(d):
        def arrive(e, _):
            wait_owner(d, e)
            return 0

        lax.fori_loop(1, BLOCKS, arrive, 0)

        def fill(e):
            base = 2 * ((t + e) % SEGS)
            for i in range(2):
                taken = recv_o[d][src_ref[base + i]]
                keep = jnp.broadcast_to(fill_ref[base + i], (TILE, TILE)) > 0
                send_t[d, e, i] = jnp.where(keep, taken.astype(jnp.float32), 0.0).astype(jnp.bfloat16)

        def send(e, _):
            fill(e)
            slot_copy(d, e).start()
            return 0

        lax.fori_loop(1, SEGS, send, 0)
        fill(0)
        own_slots(d).start()

    compute(0)
    compute(1)
    start_pieces(0)
    compute(2)
    start_owners(0)
    start_pieces(1)
    compute(3)
    start_owners(1)
    start_pieces(2)
    compute(4)
    start_slots(0)
    start_owners(2)
    start_pieces(3)
    start_slots(1)
    start_owners(3)
    start_slots(2)
    start_slots(3)

    for k in range(4):
        halo_copy(k).wait_send()
    for i in range(APER):
        following_copy(i).wait_send()
    for c in range(5):
        for k in (1, 2, 3):
            window_copy(k, c, own_tile(c)).wait_send()
        partner_power(c).wait_send()
    for d in range(4):
        for a in range(2):
            partner_terms(d, a).wait_send()
        for k in (1, 2, 3):
            piece_copy(d, k).wait_send()

        def owner_done(e, _, d=d):
            owner_copy(d, e).wait_send()
            return 0

        lax.fori_loop(1, BLOCKS, owner_done, 0)

        def slot_done(e, _, d=d):
            slot_copy(d, e).wait_send()
            wait_slots(d, e)
            return 0

        lax.fori_loop(1, SEGS, slot_done, 0)
        own_slots(d).wait()


def route(tile_owner):
    owner_table = tile_owner.reshape(BLOCKS, NT_HERE)
    my_index = lax.axis_index(("rowblk", "colblk"))
    my_owners = lax.dynamic_index_in_dim(owner_table, my_index, 0, keepdims=False)
    targets = jnp.arange(BLOCKS, dtype=jnp.int32)
    matches = my_owners[None, :] == targets[:, None]
    local_pos = jnp.sum(
        jnp.where(matches, jnp.arange(NT_HERE, dtype=jnp.int32)[None, :], 0), axis=1
    )
    arrived = jnp.any(owner_table == my_index, axis=1)
    slot_rank = jnp.cumsum(arrived.astype(jnp.int32)) - 1
    picker = (slot_rank[None, :] == jnp.arange(OCAP, dtype=jnp.int32)[:, None]) & arrived[None, :]
    source_of = jnp.sum(jnp.where(picker, targets[None, :], 0), axis=1)
    filled = jnp.any(picker, axis=1).astype(jnp.int32)
    return local_pos, source_of, filled


NT_HERE = 8


def shards(signal, tile_owner):
    local_pos, source_of, filled = route(tile_owner)
    bf16, f32, vmem, dma = jnp.bfloat16, jnp.float32, pltpu.VMEM, pltpu.SemaphoreType.DMA
    out = pl.pallas_call(
        kernel,
        out_shape=jax.ShapeDtypeStruct((2, LAGS, TILE, WIN), bf16),
        in_specs=[pl.BlockSpec(memory_space=pltpu.SMEM)] * 3 + [pl.BlockSpec(memory_space=pl.ANY)],
        out_specs=pl.BlockSpec(memory_space=pl.ANY),
        scratch_shapes=[
            vmem((4, ROWS, 5 * TILE), bf16),
            vmem((4, HALO, HALF), bf16),
            vmem((APER, ROWS, TILE), bf16),
            vmem((4, 2, LAGS * TILE, ROWS), bf16),
            vmem((4, 2, LAGS, TILE, TILE), f32),
            vmem((5, 8, TILE), f32),
            vmem((5, 8, TILE), f32),
            vmem((2, TILE, TILE), f32),
            vmem((4, 2, 4, TILE, TILE), bf16),
            vmem((4, 2, 4, TILE, TILE), bf16),
            vmem((4, 4, 2, TILE, TILE), bf16),
        ]
        + [vmem((8, TILE, TILE), bf16)] * 4
        + [vmem((BLOCKS, TILE, TILE), bf16)] * 4
        + [
            vmem((4, BLOCKS, TILE, TILE), bf16),
            vmem((4, SEGS, 2, TILE, TILE), bf16),
            dma((4, 5)), dma((4, 5)), dma((3,)), dma((3,)), dma((4,)), dma((4,)), dma((5,)), dma((5,)), dma((4, 2)), dma((4, 2)),
            dma((4, 4)), dma((4, 4)), dma((4, BLOCKS)), dma((4, BLOCKS)), dma((4, SEGS)), dma((4, SEGS)),
        ],
        compiler_params=pltpu.CompilerParams(
            collective_id=0, has_side_effects=True, vmem_limit_bytes=48 * 1024 * 1024
        ),
    )(local_pos, source_of, filled, signal)
    return out.astype(f32)[None]


def solution(mesh):
    return jax.shard_map(
        shards,
        mesh=mesh,
        in_specs=(P("tm", ("rowblk", "colblk")), P()),
        out_specs=P(("rowblk", "colblk"), "tm", None, None, None),
        check_vma=False,
    )
```

```python
import functools

import jax
import jax.numpy as jnp
from jax import lax
from jax.experimental import pallas as pl
from jax.experimental.pallas import tpu as pltpu
from jax.sharding import PartitionSpec as P

MESH = pl.DeviceIdType.MESH
TILE = 128
LAGS = 8
APER = 3
OCAP = 16
BLOCKS = 16
SEGS = 8
ROWS = 768
WIN = 512
HALF = 256
HALO = 16
PRESCALE = 2.0**40
FIRST_SENDS = ((2, 0), (1, 0), (3, 0), (2, 1), (1, 1), (3, 1))
LATER_SENDS = (
    ((2, 2), (1, 2), (3, 2), (0, 2)), ((2, 3), (1, 3), (3, 3), (0, 3)), ((2, 4), (1, 4), (3, 4), (0, 4)), (), (),
)


def kernel(
    pos_ref, src_ref, fill_ref, sig_ref, out_ref,
    ybuf, halo, following, amat, acc, pow_mine, pow_other, row_scale, send_y, recv_y, send_z,
    piece_0, piece_1, piece_2, piece_3, recv_o_0, recv_o_1, recv_o_2, recv_o_3, send_o, send_t,
    g_send, g_recv, n_send, n_recv, h_send, h_recv, p_send, p_recv, y_send, y_recv,
    z_send, z_recv, o_send, o_recv, t_send, t_recv,
):
    t = lax.axis_index("tm")
    row = lax.axis_index("rowblk")
    col = lax.axis_index("colblk")
    b = row * 4 + col
    z = t // 2
    yl = t % 2
    piece = (piece_0, piece_1, piece_2, piece_3)
    recv_o = (recv_o_0, recv_o_1, recv_o_2, recv_o_3)

    def dev(block, tm):
        return (tm, block // 4, block % 4)

    def remote(src, dst, send_sem, recv_sem, device):
        return pltpu.make_async_remote_copy(
            src_ref=src, dst_ref=dst, send_sem=send_sem, recv_sem=recv_sem,
            device_id=device, device_id_type=MESH,
        )

    partner = dev(b, 2 * z + 1 - yl)

    barrier = pltpu.get_barrier_semaphore()
    for d in range(1, SEGS):
        pl.semaphore_signal(barrier, inc=1, device_id=dev(b, (t + d) % SEGS), device_id_type=MESH)
    for d in range(1, BLOCKS):
        pl.semaphore_signal(barrier, inc=1, device_id=dev((b + d) % BLOCKS, t), device_id_type=MESH)

    def window_dst(c):
        return ybuf.at[z, :, pl.ds(c * TILE, TILE)]

    def own_tile(g):
        return sig_ref.at[:, pl.ds(pl.multiple_of(g * TILE, TILE), TILE)]

    def window_copy(k, c, src):
        zd = (z + k) % 4
        return remote(src, window_dst(c), g_send.at[k, c], g_recv.at[z, c], dev(b, 2 * zd + yl))

    def start_window(k, c):
        g = 2 * ((z + k) % 4) + c

        def start(src):
            if k == 0:
                pltpu.make_async_copy(src, window_dst(c), g_recv.at[z, c]).start()
            else:
                window_copy(k, c, src).start()

        if c < 2:
            start(own_tile(g))
        else:
            pl.when(g < 8)(lambda: start(own_tile(g)))
            pl.when(g >= 8)(lambda: start(following.at[g - 8]))

    def wait_window(k, c):
        s = (z + k) % 4
        dst = ybuf.at[s, :, pl.ds(c * TILE, TILE)]
        if k == 0:
            pltpu.make_async_copy(dst, dst, g_recv.at[s, c]).wait()
        else:
            remote(dst, dst, g_send.at[k, c], g_recv.at[s, c], partner).wait_recv()

    def following_copy(i):
        return remote(
            own_tile(i), following.at[i], n_send.at[i], n_recv.at[i], dev((b + BLOCKS - 1) % BLOCKS, t)
        )

    def halo_copy(k):
        zd = (z + k) % 4
        slot = (z + yl) % 4
        src = sig_ref.at[pl.ds(ROWS - HALO, HALO), pl.ds(pl.multiple_of(zd * HALF, HALF), HALF)]
        return remote(src, halo.at[slot], h_send.at[k], h_recv.at[slot], dev(b, 2 * zd + 1 - yl))

    def wait_halo(s):
        remote(halo.at[s], halo.at[s], h_send.at[0], h_recv.at[s], partner).wait_recv()

    for c in range(2):
        start_window(0, c)

    pl.semaphore_wait(barrier, SEGS - 1 + BLOCKS - 1)

    for k in range(4):
        halo_copy(k).start()
    for i in range(APER):
        following_copy(i).start()
    for k, c in FIRST_SENDS:
        start_window(k, c)

    def square_sums(s, c, first):
        v = ybuf[s, :, c * TILE : (c + 1) * TILE].astype(jnp.float32)
        total = jnp.sum((v * v).reshape(ROWS // 8, 8, TILE), axis=0)
        pow_mine[c] = total if first else pow_mine[c] + total

    def build_lags(s, a):
        keep = jnp.where(jnp.logical_and(s == 0, yl == 0), 0.0, PRESCALE)
        x = ybuf[s, :, a * TILE : (a + 1) * TILE].astype(jnp.float32) * PRESCALE
        h = halo[s, :, a * TILE : (a + 1) * TILE].astype(jnp.float32) * keep
        rows = jnp.concatenate([jnp.zeros((TILE - HALO, TILE), jnp.float32), h, x], axis=0)
        cols = jnp.transpose(rows)
        for j in range(LAGS):
            shifted = cols if j == 0 else pltpu.roll(cols, j, 1)
            amat[s, a, j * TILE : (j + 1) * TILE, :] = shifted[:, TILE:].astype(jnp.bfloat16)

    def products(s, c, first):
        y = ybuf[s, :, c * TILE : (c + 1) * TILE]
        for a in range(2):
            d = c - a
            if 0 <= d < 4:
                for j in range(0, LAGS, 4):
                    p = jnp.dot(
                        amat[s, a, j * TILE : (j + 4) * TILE, :], y, preferred_element_type=jnp.float32
                    ).reshape(4, TILE, TILE)
                    acc[d, a, j : j + 4] = p if first else acc[d, a, j : j + 4] + p

    def partner_power(c):
        return remote(pow_mine.at[c], pow_other.at[c], p_send.at[c], p_recv.at[c], partner)

    def partner_terms(d, a):
        return remote(send_y.at[d, a], recv_y.at[d, a], y_send.at[d, a], y_recv.at[d, a], partner)

    def compute(c):
        for k in (0, 1, 3, 2):
            s = (z + k) % 4
            if c == 0:
                wait_halo(s)
            wait_window(k, c)
            if c < 2:
                build_lags(s, c)
            products(s, c, k == 0)
            square_sums(s, c, k == 0)
        if c == 0:
            for i in range(APER):
                following_copy(i).wait_recv()
        for k, e in LATER_SENDS[c]:
            start_window(k, e)
        partner_power(c).start()
        for a in range(2):
            d = c - a
            if 0 <= d < 4:
                for q in range(4):
                    send_y[d, a, q] = acc[d, a, 2 * q + 1 - yl].astype(jnp.bfloat16)
                partner_terms(d, a).start()

    def channel_scale(c):
        total = jnp.sum(pow_mine[c] + pow_other[c], axis=0, keepdims=True)
        return lax.rsqrt(total * (1.0 / (SEGS * ROWS)) + 1e-06)

    def piece_copy(d, k):
        zd = (z + k) % 4
        return remote(
            send_z.at[d, zd], piece[d].at[pl.ds(2 * z, 2)], z_send.at[d, k], z_recv.at[d, z],
            dev(b, 2 * zd + yl),
        )

    def wait_piece(d, k):
        s = (z + k) % 4
        remote(
            send_z.at[d, s], piece[d].at[pl.ds(2 * s, 2)], z_send.at[d, k], z_recv.at[d, s], partner
        ).wait_recv()

    def start_pieces(d):
        if d == 0:
            norm = (1.0 / PRESCALE) * float(SEGS * ROWS) ** -0.5
            for a in range(2):
                partner_power(a).wait_recv()
                row_scale[a] = jnp.transpose(jnp.broadcast_to(channel_scale(a) * norm, (TILE, TILE)))
        else:
            partner_power(d + 1).wait_recv()
        for a in range(2):
            outside = jnp.logical_and(2 * z + d + a >= 8, b == BLOCKS - 1)
            both = row_scale[a] * (channel_scale(d + a) * jnp.where(outside, 0.0, 1.0))
            partner_terms(d, a).wait_recv()
            for q in range(4):
                total = acc[d, a, 2 * q + yl] + recv_y[d, a, q].astype(jnp.float32)
                send_z[d, q, a] = (total * both).astype(jnp.bfloat16)
        for k in (2, 1, 3):
            piece_copy(d, k).start()
        piece[d][pl.ds(2 * z, 2)] = send_z[d, z]

    def owner_copy(d, e):
        o = (b + e) % BLOCKS
        return remote(send_o.at[d, e], recv_o[d].at[b], o_send.at[d, e], o_recv.at[d, b], dev(o, t))

    def wait_owner(d, e):
        s = (b + e) % BLOCKS
        remote(send_o.at[d, e], recv_o[d].at[s], o_send.at[d, e], o_recv.at[d, s], partner).wait_recv()

    def start_owners(d):
        for k in (1, 3, 2):
            wait_piece(d, k)

        def send(i, _):
            e = (i * 3) % BLOCKS
            send_o[d, e] = piece[d][pos_ref[(b + e) % BLOCKS]]
            owner_copy(d, e).start()
            return 0

        lax.fori_loop(1, BLOCKS, send, 0)
        recv_o[d][b] = piece[d][pos_ref[b]]

    def slot_dst(d, lag):
        return out_ref.at[:, lag, :, pl.ds(d * TILE, TILE)]

    def slot_copy(d, e):
        return remote(
            send_t.at[d, e], slot_dst(d, t), t_send.at[d, e], t_recv.at[d, t],
            dev(b, (t + e) % SEGS),
        )

    def own_slots(d):
        return pltpu.make_async_copy(send_t.at[d, 0], slot_dst(d, t), t_recv.at[d, t])

    def wait_slots(d, e):
        s = (t + e) % SEGS
        remote(send_t.at[d, e], slot_dst(d, s), t_send.at[d, e], t_recv.at[d, s], partner).wait_recv()

    def start_slots(d):
        def arrive(e, _):
            wait_owner(d, e)
            return 0

        lax.fori_loop(1, BLOCKS, arrive, 0)

        def fill(e):
            base = 2 * ((t + e) % SEGS)
            for i in range(2):
                taken = recv_o[d][src_ref[base + i]]
                keep = jnp.broadcast_to(fill_ref[base + i], (TILE, TILE)) > 0
                send_t[d, e, i] = jnp.where(keep, taken.astype(jnp.float32), 0.0).astype(jnp.bfloat16)

        def send(e, _):
            fill(e)
            slot_copy(d, e).start()
            return 0

        lax.fori_loop(1, SEGS, send, 0)
        fill(0)
        own_slots(d).start()

    compute(0)
    compute(1)
    start_pieces(0)
    compute(2)
    start_owners(0)
    start_pieces(1)
    compute(3)
    start_owners(1)
    start_pieces(2)
    compute(4)
    start_owners(2)
    start_slots(0)
    start_pieces(3)
    start_owners(3)
    start_slots(1)
    start_slots(2)
    start_slots(3)

    for k in range(4):
        halo_copy(k).wait_send()
    for i in range(APER):
        following_copy(i).wait_send()
    for c in range(5):
        for k in (1, 2, 3):
            window_copy(k, c, own_tile(c)).wait_send()
        partner_power(c).wait_send()
    for d in range(4):
        for a in range(2):
            partner_terms(d, a).wait_send()
        for k in (1, 2, 3):
            piece_copy(d, k).wait_send()

        def owner_done(e, _, d=d):
            owner_copy(d, e).wait_send()
            return 0

        lax.fori_loop(1, BLOCKS, owner_done, 0)

        def slot_done(e, _, d=d):
            slot_copy(d, e).wait_send()
            wait_slots(d, e)
            return 0

        lax.fori_loop(1, SEGS, slot_done, 0)
        own_slots(d).wait()


def route(tile_owner):
    owner_table = tile_owner.reshape(BLOCKS, NT_HERE)
    my_index = lax.axis_index(("rowblk", "colblk"))
    my_owners = lax.dynamic_index_in_dim(owner_table, my_index, 0, keepdims=False)
    targets = jnp.arange(BLOCKS, dtype=jnp.int32)
    matches = my_owners[None, :] == targets[:, None]
    local_pos = jnp.sum(
        jnp.where(matches, jnp.arange(NT_HERE, dtype=jnp.int32)[None, :], 0), axis=1
    )
    arrived = jnp.any(owner_table == my_index, axis=1)
    slot_rank = jnp.cumsum(arrived.astype(jnp.int32)) - 1
    picker = (slot_rank[None, :] == jnp.arange(OCAP, dtype=jnp.int32)[:, None]) & arrived[None, :]
    source_of = jnp.sum(jnp.where(picker, targets[None, :], 0), axis=1)
    filled = jnp.any(picker, axis=1).astype(jnp.int32)
    return local_pos, source_of, filled


NT_HERE = 8


def shards(signal, tile_owner):
    local_pos, source_of, filled = route(tile_owner)
    bf16, f32, vmem, dma = jnp.bfloat16, jnp.float32, pltpu.VMEM, pltpu.SemaphoreType.DMA
    out = pl.pallas_call(
        kernel,
        out_shape=jax.ShapeDtypeStruct((2, LAGS, TILE, WIN), bf16),
        in_specs=[pl.BlockSpec(memory_space=pltpu.SMEM)] * 3 + [pl.BlockSpec(memory_space=pl.ANY)],
        out_specs=pl.BlockSpec(memory_space=pl.ANY),
        scratch_shapes=[
            vmem((4, ROWS, 5 * TILE), bf16),
            vmem((4, HALO, HALF), bf16),
            vmem((APER, ROWS, TILE), bf16),
            vmem((4, 2, LAGS * TILE, ROWS), bf16),
            vmem((4, 2, LAGS, TILE, TILE), f32),
            vmem((5, 8, TILE), f32),
            vmem((5, 8, TILE), f32),
            vmem((2, TILE, TILE), f32),
            vmem((4, 2, 4, TILE, TILE), bf16),
            vmem((4, 2, 4, TILE, TILE), bf16),
            vmem((4, 4, 2, TILE, TILE), bf16),
        ]
        + [vmem((8, TILE, TILE), bf16)] * 4
        + [vmem((BLOCKS, TILE, TILE), bf16)] * 4
        + [
            vmem((4, BLOCKS, TILE, TILE), bf16),
            vmem((4, SEGS, 2, TILE, TILE), bf16),
            dma((4, 5)), dma((4, 5)), dma((3,)), dma((3,)), dma((4,)), dma((4,)), dma((5,)), dma((5,)), dma((4, 2)), dma((4, 2)),
            dma((4, 4)), dma((4, 4)), dma((4, BLOCKS)), dma((4, BLOCKS)), dma((4, SEGS)), dma((4, SEGS)),
        ],
        compiler_params=pltpu.CompilerParams(
            collective_id=0, has_side_effects=True, vmem_limit_bytes=48 * 1024 * 1024
        ),
    )(local_pos, source_of, filled, signal)
    return out.astype(f32)[None]


def solution(mesh):
    return jax.shard_map(
        shards,
        mesh=mesh,
        in_specs=(P("tm", ("rowblk", "colblk")), P()),
        out_specs=P(("rowblk", "colblk"), "tm", None, None, None),
        check_vma=False,
    )
```
